128 devices in a mesh: grp: 8 (over z, core), blk: 16 (over x, y).
Axes of the slice: x: 4, y: 4, z: 4, core: 2. Of those that a mesh axis runs over, the one named last changes fastest.
Arguments:
- left_tensor: bfloat16 [8, 3072, 768], P('grp', 'blk'), may hold values from -6 to 6
- right_tensor: bfloat16 [8, 768, 3072], P('grp', 'blk'), may hold values from -0.21875 to 0.21875
- diag_gate: float32 [8, 3072], P('grp'), may hold values from 0.2 to 1
- hop_gate: float32 [8, 3072], P('grp'), may hold values from -0.6 to 0.6
- sketch: bfloat16 [3072, 768], replicated, may hold values from -0.109375 to 0.109375
- sector_rows: int32 [8], P('grp'), may hold values from 1536 to 3072, as said below
- kept: int32 [8], P('grp'), may hold values from 384 to 768, as said below
Outputs:
- left_out: float32 [8, 3072, 768], P('grp', 'blk')
- right_out: float32 [3072, 8, 768], P('blk', 'grp')
The draws below stay inside these ranges and needn't reach their ends.
Inputs may be any that keep to these rules, and one draw needn't show every extreme that they name: `sector_rows`: reached by some sector in every draw, at both ends. `kept`: reached by some sector in every draw, at both ends.
All inputs are finite; a program needn't handle non-finite values.
Results may differ from the reference program's by a relative error of at most 0.022.
Values may be sent and summed in bfloat16 or wider, within the bound.
A program may use at most 128 MiB of HBM per device.

```python
import math
import jax
import jax.numpy as jnp
from jax import lax

R = 3072
X = 768
C = 3072
K = 768
SECTORS = 8


def draw_sector_rows(key, part):
    values = jax.random.randint(jax.random.fold_in(key, 11), (SECTORS,), R // 2, R + 1)
    first = jax.random.randint(jax.random.fold_in(key, 12), (), 0, SECTORS)
    second = (first + 1) % SECTORS
    values = values.at[first].set(R)
    values = values.at[second].set(R // 2)
    return values.astype(jnp.int32)


def draw_kept(key, part):
    values = jax.random.randint(jax.random.fold_in(key, 21), (SECTORS,), K // 2, K + 1)
    first = jax.random.randint(jax.random.fold_in(key, 22), (), 0, SECTORS)
    second = (first + 1) % SECTORS
    values = values.at[first].set(K)
    values = values.at[second].set(K // 2)
    return values.astype(jnp.int32)


def level_of(stream_key, extent, pieces, smallest, high):
    def one(dim, parts):
        draws = jax.random.uniform(jax.random.fold_in(jax.random.fold_in(stream_key, 6), dim), (parts,), jnp.float32, smallest / len(pieces), high / len(pieces))
        return jnp.repeat(jnp.exp(draws), extent[dim] // parts).reshape((-1,) + (1,) * (len(extent) - dim - 1))

    gain = one(*pieces[0])
    for cut in pieces[1:]:
        gain = gain * one(*cut)
    return gain


def bell_draw(own_key, shape, width, most, cuts=(), held_as=jnp.bfloat16):
    array = jax.random.normal(own_key, shape, jnp.float32) * width
    if len(cuts) > 0:
        array = level_of(own_key, shape, cuts, -0.22, 0.18) * array
    return jnp.clip(array, min=-most, max=most).astype(held_as)


def setup_inputs(seed: int = 0) -> dict:
    keys = jax.random.split(jax.random.key(seed), 8)
    return {
        "left_tensor": bell_draw(keys[0], (SECTORS, R, X), 1.0, 6.0, ((0, 8), (1, 16))),
        "right_tensor": bell_draw(keys[1], (SECTORS, X, C), X ** -0.5, 0.21875, ((0, 8), (1, 16))),
        "diag_gate": jnp.clip(jnp.exp(math.log(1.0) - 1.609438 * jax.random.uniform(keys[2], (SECTORS, C), jnp.float32) ** level_of(keys[2], (SECTORS, C), ((0, 8),), -0.2, 0.2)), 0.2, 1.0),
        "hop_gate": jnp.clip(jax.random.uniform(keys[3], (SECTORS, C), jnp.float32, -0.6, 0.6) * level_of(keys[3], (SECTORS, C), ((0, 8),), -0.4, 0.0), -0.6, 0.6),
        "sketch": bell_draw(keys[4], (C, K), C ** -0.5, 0.109375),
        "sector_rows": draw_sector_rows(jax.random.fold_in(keys[7], 71), 0),
        "kept": draw_kept(jax.random.fold_in(keys[7], 71), 0),
    }


def reference(left_tensor, right_tensor, diag_gate, hop_gate, sketch, sector_rows, kept):
    high = lax.Precision.HIGHEST
    theta_full = jnp.einsum('srx,sxc->src', left_tensor.astype(jnp.float32), right_tensor.astype(jnp.float32), precision=high).astype(jnp.bfloat16)
    theta_wide = theta_full.astype(jnp.float32)
    zero_block = jnp.zeros_like(theta_wide[:1])
    below = jnp.concatenate([zero_block, theta_wide[:-1]], axis=0)
    above = jnp.concatenate([theta_wide[1:], zero_block], axis=0)
    mixed_wide = diag_gate[:, None, :] * theta_wide + hop_gate[:, None, :] * (below + above)
    row_live = (jnp.arange(R, dtype=jnp.int32)[None, :] < sector_rows[:, None]).astype(jnp.float32)
    mixed_b = (mixed_wide * row_live[:, :, None]).astype(jnp.bfloat16)
    col_live = (jnp.arange(K, dtype=jnp.int32)[None, :] < kept[:, None]).astype(jnp.float32)
    sketched = jnp.einsum('src,ck->srk', mixed_b.astype(jnp.float32), sketch.astype(jnp.float32), precision=high)
    sketched = (sketched * col_live[:, None, :]).astype(jnp.bfloat16)
    sketch_wide = sketched.astype(jnp.float32)
    gram_mat = jnp.einsum('srk,srj->skj', sketch_wide, sketch_wide, precision=high)
    gram_mat = gram_mat + (1.0 - col_live)[:, :, None] * jnp.eye(K, dtype=jnp.float32)[None]
    factor = jnp.linalg.cholesky(gram_mat)
    ortho_basis = lax.linalg.triangular_solve(factor, sketch_wide, left_side=False, lower=True, transpose_a=True)
    row_scale = math.sqrt(R)
    left_out = ortho_basis * row_scale
    basis_b = ortho_basis.astype(jnp.bfloat16)
    right_out = jnp.einsum('src,srk->csk', mixed_b.astype(jnp.float32), basis_b.astype(jnp.float32), precision=high) / row_scale
    return (left_out, right_out)
```

```python
import math

import jax
import jax.numpy as jnp
from jax import lax
from jax.experimental import pallas as pl
from jax.experimental.pallas import tpu as pltpu
from jax.sharding import PartitionSpec as P

HIGH = lax.Precision.HIGHEST
B = 128


def reciprocal(p):
    r = pl.reciprocal(p, approx=True)
    return r * (2.0 - p * r)


def pivot_inverse(a):
    lane = lax.broadcasted_iota(jnp.int32, (8, B), 1)
    sub = lax.broadcasted_iota(jnp.int32, (8, B), 0)
    n = B // 8
    rows = [a[8 * i : 8 * i + 8] for i in range(n)]
    out = []
    wide = lambda x: jnp.broadcast_to(x, (8, B))
    for q in range(n):
        k = 8 * q
        cols = [wide(rows[q][:, k + t : k + t + 1]) for t in range(8)]
        piv = [[wide(cols[j][i : i + 1, :]) if j <= i else None for j in range(8)] for i in range(8)]
        inside = (lane >= k) & (lane < k + 8)
        e = [
            jnp.where(lane == k + t, 1.0, jnp.where(inside, 0.0, wide(rows[q][t : t + 1, :])))
            for t in range(8)
        ]
        fin, s, u, ds = [None] * 8, [None] * 8, {}, []
        for t in range(0, 8, 2):
            p0, p1, p2 = piv[t][t], piv[t + 1][t], piv[t + 1][t + 1]
            rd = reciprocal(p0 * p2 - p1 * p1)
            i0, i1, i2 = p2 * rd, p1 * rd, p0 * rd
            ds.append((i0, i1, i2))
            for i in range(t + 2, 8):
                x0, x1 = piv[i][t], piv[i][t + 1]
                u[i, t] = x0 * i0 - x1 * i1
                u[i, t + 1] = x1 * i2 - x0 * i1
            for i in range(t + 2, 8):
                for j in range(t + 2, i + 1):
                    piv[i][j] = piv[i][j] - (u[i, t] * piv[j][t] + u[i, t + 1] * piv[j][t + 1])
                e[i] = e[i] - (u[i, t] * e[t] + u[i, t + 1] * e[t + 1])
            ra = lax.rsqrt(p0)
            m = p1 * ra * ra
            fin[t] = e[t] * ra
            fin[t + 1] = (e[t + 1] - m * e[t]) * lax.rsqrt(p2 - m * p1)
        if q < n - 1:
            for t in range(6, -1, -2):
                i0, i1, i2 = ds[t // 2]
                v0 = e[t] * i0 - e[t + 1] * i1
                v1 = e[t + 1] * i2 - e[t] * i1
                for i in range(7, t + 1, -1):
                    v0 = v0 - u[i, t] * s[i]
                    v1 = v1 - u[i, t + 1] * s[i]
                s[t], s[t + 1] = v0, v1
        o = fin[0]
        for t in range(1, 8):
            o = jnp.where(sub == t, fin[t], o)
        out.append(jnp.where(lane <= sub + k, o, 0.0))
        for i in range(q + 1, n):
            acc = jnp.where(inside, 0.0, rows[i])
            for t in range(8):
                acc = acc - wide(rows[i][:, k + t : k + t + 1]) * s[t]
            rows[i] = acc
    return jnp.concatenate(out, axis=0)


def factor_inverse_kernel(n, g_ref, w):
    w[...] = g_ref[...]

    def step(j, carry):
        jj = pl.multiple_of(j * B, B)
        inv = pivot_inverse(w[pl.ds(jj, B), pl.ds(jj, B)])
        w[pl.ds(jj, B), :] = jnp.dot(
            inv, w[pl.ds(jj, B), :], precision=HIGH, preferred_element_type=jnp.float32
        )
        w[pl.ds(jj, B), pl.ds(jj, B)] = inv

        def update(i, c):
            ii = pl.multiple_of(i * B, B)
            m = w[pl.ds(jj, B), pl.ds(ii, B)]
            w[pl.ds(ii, B), pl.ds(jj, B)] = jnp.zeros((B, B), jnp.float32)
            w[pl.ds(ii, B), :] = w[pl.ds(ii, B), :] - lax.dot_general(
                m,
                w[pl.ds(jj, B), :],
                (((0,), (0,)), ((), ())),
                precision=HIGH,
                preferred_element_type=jnp.float32,
            )
            return c

        lax.fori_loop(j + 1, n, update, 0)
        return carry

    lax.fori_loop(0, n, step, 0)
    for j in range(n - 1):
        w[j * B : (j + 1) * B, (j + 1) * B :] = jnp.zeros((B, (n - 1 - j) * B), jnp.float32)


def factor_inverse(gram):
    k = gram.shape[0]
    return pl.pallas_call(
        lambda *refs: factor_inverse_kernel(k // B, *refs),
        out_shape=jax.ShapeDtypeStruct((k, k), jnp.float32),
        in_specs=[pl.BlockSpec(memory_space=pltpu.VMEM)],
        out_specs=pl.BlockSpec(memory_space=pltpu.VMEM),
        compiler_params=pltpu.CompilerParams(vmem_limit_bytes=24 * 2**20),
        cost_estimate=pl.CostEstimate(flops=8 * 10**9, bytes_accessed=10**8, transcendentals=0),
    )(gram)


def dot32(a, b, dims, **kw):
    return lax.dot_general(a, b, (dims, ((), ())), preferred_element_type=jnp.float32, **kw)


def body(left_tensor, right_tensor, diag_gate, hop_gate, sketch, sector_rows, kept):
    bf16, f32 = jnp.bfloat16, jnp.float32
    left, right, diag, hop = left_tensor[0], right_tensor[0], diag_gate[0], hop_gate[0]
    rows_here, middle = left.shape
    width = sketch.shape[1]
    columns = right.shape[1]
    blk_count = lax.axis_size("blk")
    total = rows_here * blk_count
    cols_here = columns // blk_count
    groups = lax.axis_size("grp")
    me = lax.axis_index("blk")
    up = [(i, i + 1) for i in range(groups - 1)]
    down = [(i + 1, i) for i in range(groups - 1)]
    low = lambda x: lax.ppermute(x, "grp", up)
    high = lambda x: lax.ppermute(x, "grp", down)

    right_low, right_high = low(right), high(right)
    left_low, left_high = low(left), high(left)
    stack = jnp.concatenate(
        [
            right.astype(f32) * diag[None],
            right_low.astype(f32) * hop[None],
            right_high.astype(f32) * hop[None],
        ],
        axis=0,
    ).astype(bf16)
    mapped = dot32(stack, sketch, ((1,), (0,))).astype(bf16)
    mapped = lax.all_gather(mapped.reshape(3, -1, width), "blk", axis=1, tiled=True)
    wide_left = jnp.concatenate([left, left_low, left_high], axis=1)
    sketched = dot32(wide_left, mapped.reshape(-1, width), ((1,), (0,)))
    row_index = me * rows_here + jnp.arange(rows_here, dtype=jnp.int32)
    live = row_index[:, None] < sector_rows[0]
    col_live = jnp.arange(width, dtype=jnp.int32)[None, :] < kept[0]
    sketched = jnp.where(live & col_live, sketched, 0.0).astype(bf16)
    sketched_all = lax.all_gather(sketched, "blk", axis=0, tiled=True)
    gram = dot32(sketched_all, sketched_all, ((0,), (0,)))
    gram = gram + jnp.where(col_live, 0.0, 1.0) * jnp.eye(width, dtype=f32)

    left_all = lax.all_gather(left, "blk", axis=0, tiled=True)
    right_c = lax.all_to_all(right, "blk", split_axis=1, concat_axis=0, tiled=True)
    theta_c = dot32(left_all, right_c, ((1,), (0,))).astype(bf16)
    theta_low, theta_high = low(theta_c).astype(f32), high(theta_c).astype(f32)
    diag_c = lax.dynamic_slice_in_dim(diag, me * cols_here, cols_here)
    hop_c = lax.dynamic_slice_in_dim(hop, me * cols_here, cols_here)
    mixed_c = diag_c[None] * theta_c.astype(f32) + hop_c[None] * (theta_low + theta_high)
    all_live = jnp.arange(total, dtype=jnp.int32)[:, None] < sector_rows[0]
    mixed_c = jnp.where(all_live, mixed_c, 0.0).astype(bf16)
    projected = dot32(mixed_c, sketched_all, ((0,), (0,)))

    inverse = factor_inverse(gram)
    scale = math.sqrt(total)
    left_out = dot32(sketched.astype(f32), inverse, ((1,), (1,)), precision=HIGH) * scale
    right_out = dot32(projected, inverse, ((1,), (1,)), precision=HIGH) / scale
    return (left_out[None], right_out[:, None, :])


def solution(mesh):
    in_specs = (
        P("grp", "blk", None),
        P("grp", "blk", None),
        P("grp", None),
        P("grp", None),
        P(),
        P("grp"),
        P("grp"),
    )
    out_specs = (P("grp", "blk", None), P("blk", "grp", None))
    return jax.shard_map(body, mesh=mesh, in_specs=in_specs, out_specs=out_specs, check_vma=False)
```

```python
import math

import jax
import jax.numpy as jnp
from jax import lax
from jax.experimental import pallas as pl
from jax.experimental.pallas import tpu as pltpu
from jax.sharding import PartitionSpec as P

HIGH = lax.Precision.HIGHEST
B = 128


def reciprocal(p):
    r = pl.reciprocal(p, approx=True)
    return r * (2.0 - p * r)


def pivot_inverse(a):
    lane = lax.broadcasted_iota(jnp.int32, (8, B), 1)
    sub = lax.broadcasted_iota(jnp.int32, (8, B), 0)
    n = B // 8
    rows = [a[8 * i : 8 * i + 8] for i in range(n)]
    out = []
    wide = lambda x: jnp.broadcast_to(x, (8, B))
    for q in range(n):
        k = 8 * q
        cols = [wide(rows[q][:, k + t : k + t + 1]) for t in range(8)]
        piv = [[wide(cols[j][i : i + 1, :]) if j <= i else None for j in range(8)] for i in range(8)]
        inside = (lane >= k) & (lane < k + 8)
        e = [
            jnp.where(lane == k + t, 1.0, jnp.where(inside, 0.0, wide(rows[q][t : t + 1, :])))
            for t in range(8)
        ]
        fin, s, u, ds = [None] * 8, [None] * 8, {}, []
        for t in range(0, 8, 2):
            p0, p1, p2 = piv[t][t], piv[t + 1][t], piv[t + 1][t + 1]
            rd = reciprocal(p0 * p2 - p1 * p1)
            i0, i1, i2 = p2 * rd, p1 * rd, p0 * rd
            ds.append((i0, i1, i2))
            for i in range(t + 2, 8):
                x0, x1 = piv[i][t], piv[i][t + 1]
                u[i, t] = x0 * i0 - x1 * i1
                u[i, t + 1] = x1 * i2 - x0 * i1
            for i in range(t + 2, 8):
                for j in range(t + 2, i + 1):
                    piv[i][j] = piv[i][j] - (u[i, t] * piv[j][t] + u[i, t + 1] * piv[j][t + 1])
                e[i] = e[i] - (u[i, t] * e[t] + u[i, t + 1] * e[t + 1])
            ra = lax.rsqrt(p0)
            m = p1 * ra * ra
            fin[t] = e[t] * ra
            fin[t + 1] = (e[t + 1] - m * e[t]) * lax.rsqrt(p2 - m * p1)
        if q < n - 1:
            for t in range(6, -1, -2):
                i0, i1, i2 = ds[t // 2]
                v0 = e[t] * i0 - e[t + 1] * i1
                v1 = e[t + 1] * i2 - e[t] * i1
                for i in range(7, t + 1, -1):
                    v0 = v0 - u[i, t] * s[i]
                    v1 = v1 - u[i, t + 1] * s[i]
                s[t], s[t + 1] = v0, v1
        o = fin[0]
        for t in range(1, 8):
            o = jnp.where(sub == t, fin[t], o)
        out.append(jnp.where(lane <= sub + k, o, 0.0))
        for i in range(q + 1, n):
            acc = jnp.where(inside, 0.0, rows[i])
            for t in range(8):
                acc = acc - wide(rows[i][:, k + t : k + t + 1]) * s[t]
            rows[i] = acc
    return jnp.concatenate(out, axis=0)


def factor_inverse_kernel(n, s_ref, dead_ref, w):
    eye = lax.broadcasted_iota(jnp.int32, (B, B), 0) == lax.broadcasted_iota(jnp.int32, (B, B), 1)
    for j in range(n):
        if j:
            w[j * B : (j + 1) * B, : j * B] = jnp.zeros((B, j * B), jnp.float32)
        block = s_ref[:, j * B : (j + 1) * B]

        def gram(i, c, block=block):
            ii = pl.multiple_of(i * B, B)
            w[pl.ds(j * B, B), pl.ds(ii, B)] = lax.dot_general(
                block,
                s_ref[:, pl.ds(ii, B)],
                (((0,), (0,)), ((), ())),
                preferred_element_type=jnp.float32,
            )
            return c

        lax.fori_loop(j, n, gram, 0)
        here = slice(j * B, (j + 1) * B)
        w[here, here] = w[here, here] + jnp.where(eye, dead_ref[:, here], 0.0)

    def step(j, carry):
        jj = pl.multiple_of(j * B, B)
        inv = pivot_inverse(w[pl.ds(jj, B), pl.ds(jj, B)])
        w[pl.ds(jj, B), :] = jnp.dot(
            inv, w[pl.ds(jj, B), :], precision=HIGH, preferred_element_type=jnp.float32
        )
        w[pl.ds(jj, B), pl.ds(jj, B)] = inv

        def update(i, c):
            ii = pl.multiple_of(i * B, B)
            m = w[pl.ds(jj, B), pl.ds(ii, B)]
            w[pl.ds(ii, B), pl.ds(jj, B)] = jnp.zeros((B, B), jnp.float32)
            w[pl.ds(ii, B), :] = w[pl.ds(ii, B), :] - lax.dot_general(
                m,
                w[pl.ds(jj, B), :],
                (((0,), (0,)), ((), ())),
                precision=HIGH,
                preferred_element_type=jnp.float32,
            )
            return c

        lax.fori_loop(j + 1, n, update, 0)
        return carry

    lax.fori_loop(0, n, step, 0)
    for j in range(n - 1):
        w[j * B : (j + 1) * B, (j + 1) * B :] = jnp.zeros((B, (n - 1 - j) * B), jnp.float32)


def factor_inverse(sketched, dead):
    k = sketched.shape[1]
    return pl.pallas_call(
        lambda *refs: factor_inverse_kernel(k // B, *refs),
        out_shape=jax.ShapeDtypeStruct((k, k), jnp.float32),
        in_specs=[pl.BlockSpec(memory_space=pltpu.VMEM)] * 2,
        out_specs=pl.BlockSpec(memory_space=pltpu.VMEM),
        compiler_params=pltpu.CompilerParams(vmem_limit_bytes=32 * 2**20),
        cost_estimate=pl.CostEstimate(
            flops=20 * 10**9, bytes_accessed=10**8, transcendentals=0
        ),
    )(sketched, dead)


def dot32(a, b, dims, **kw):
    return lax.dot_general(a, b, (dims, ((), ())), preferred_element_type=jnp.float32, **kw)


SIDE = 4
SK_PARTS = 2


def gather_kernel(
    right, left, gates, sketch_hbm, rowm, colm, pieces,
    sk_out, pieces_out,
    sketch, mapped, right_n, left_n, total,
    load_sem, x_send, x_recv, m_send, m_recv, s_send, s_recv, a_send, a_recv, n_send, n_recv,
):
    bf16, f32 = jnp.bfloat16, jnp.float32
    g = lax.axis_index("grp")
    me = lax.axis_index("blk")
    groups = lax.axis_size("grp")
    blks = SIDE * SIDE
    cx, cy = me // SIDE, me % SIDE
    depth = right.shape[0]
    rows, width = sk_out.shape[1], sk_out.shape[2]
    half_w = width // 2

    load = pltpu.make_async_copy(sketch_hbm, sketch, load_sem)
    load.start()
    keep = pltpu.make_async_copy(pieces.at[me], pieces_out.at[0, me], a_recv.at[me])
    keep.start()

    barrier = pltpu.get_barrier_semaphore()
    peers = [{"blk": lax.rem(me + i, blks)} for i in range(1, blks)]
    up = {"grp": lax.rem(g + 1, groups)}
    down = {"grp": lax.rem(g + groups - 1, groups)}
    for peer in peers + [up, down]:
        pl.semaphore_signal(barrier, inc=1, device_id=peer, device_id_type=pl.DeviceIdType.MESH)
    pl.semaphore_wait(barrier, len(peers) + 2)

    def remote(src, dst, send, recv, to):
        return pltpu.make_async_remote_copy(
            src_ref=src, dst_ref=dst, send_sem=send, recv_sem=recv,
            device_id=to, device_id_type=pl.DeviceIdType.MESH,
        )

    started = []

    def go(copy):
        copy.start()
        started.append(copy)

    for slot, to in ((0, up), (1, down)):
        go(remote(right, right_n.at[slot], x_send.at[slot], x_recv.at[slot], to))
    for slot, to in ((0, up), (1, down)):
        go(remote(left, left_n.at[slot], x_send.at[2 + slot], x_recv.at[2 + slot], to))
    for i in range(1, blks):
        to = lax.rem(me + i, blks)
        go(remote(pieces.at[to], pieces_out.at[0, me], a_send.at[i], a_recv.at[me], {"blk": to}))

    def ring(view, send, recv):
        count = [0]

        def coords(half):
            return (cx, cy) if half == 0 else (cy, cx)

        def index(half, a, b):
            return a * SIDE + b if half == 0 else b * SIDE + a

        def owner(half, r1, r2):
            c1, c2 = coords(half)
            return index(half, lax.rem(c1 + r1, SIDE), lax.rem(c2 + r2, SIDE))

        def ship(half, block, axis, step):
            to = owner(half, step, 0) if axis == 0 else owner(half, 0, step)
            ref = view(block, half)
            go(remote(ref, ref, send.at[count[0]], recv.at[half, block], {"blk": to}))
            count[0] += 1

        def take(half, r1, r2):
            block = owner(half, r1, r2)
            ref = view(block, half)
            remote(ref, ref, send.at[0], recv.at[half, block], up).wait_recv()
            return block

        plus = (0, 3)

        def relay(half, r1):
            low = take(half, r1, 3)
            if r1 in plus:
                ship(half, low, 1, 1)
            high = take(half, r1, 1)
            if r1 not in plus:
                ship(half, high, 1, 3)

        def spread(half, block):
            ship(half, block, 1, 1)
            ship(half, block, 1, 3)

        def first():
            for half in range(2):
                ship(half, me, 0, 1)
                ship(half, me, 0, 3)
            for half in range(2):
                spread(half, me)

        def second():
            for half in range(2):
                b = take(half, 3, 0)
                if half == 0:
                    ship(half, b, 0, 1)
                spread(half, b)
                b = take(half, 1, 0)
                if half == 1:
                    ship(half, b, 0, 3)
                spread(half, b)
            for half in range(2):
                relay(half, 0)

        def third():
            for half in range(2):
                spread(half, take(half, 2, 0))
            for half in range(2):
                relay(half, 3)
                relay(half, 1)

        def fourth():
            for half in range(2):
                relay(half, 2)

        def last():
            for half in range(2):
                for r1 in (0, 3, 1, 2):
                    take(half, r1, 2)

        return first, second, third, fourth, last

    def tiles(n, f):
        lax.fori_loop(0, n, lambda i, c: (f(i), c)[1], 0)

    maps = []
    for part in range(3):
        view = lambda o, half, part=part: mapped.at[part, o, :, pl.ds(half * half_w, half_w)]
        maps.append(ring(view, m_send.at[part], m_recv.at[part]))

    def x_wait(ref, k):
        remote(ref, ref, x_send.at[k], x_recv.at[k], up).wait_recv()

    for part in range(3):
        if part == 0:
            load.wait()
            block = right[...]
        else:
            x_wait(right_n.at[part - 1], part - 1)
            block = right_n[part - 1]
        scaled = (block.astype(f32) * gates[pl.ds(part, 1), :]).astype(bf16)

        def tile(i, scaled=scaled, part=part):
            at = pl.ds(pl.multiple_of(i * 256, 256), 256)
            mapped[part, me, :, at] = jnp.dot(
                scaled, sketch[:, at], preferred_element_type=f32
            ).astype(bf16)

        tiles(width // 256, tile)
        maps[part][0]()
    for stage in range(1, 4):
        for part in range(3):
            maps[part][stage]()
    for part in range(3):
        if part == 0:
            block = left[...]
        else:
            x_wait(left_n.at[part - 1], part + 1)
            block = left_n[part - 1]
        maps[part][4]()

        def tile(i, block=block, part=part):
            at = pl.ds(pl.multiple_of(i * 256, 256), 256)
            add = jnp.dot(
                block, mapped[part, :, :, at].reshape(blks * depth, 256), preferred_element_type=f32
            )
            if part == 0:
                total[:, at] = add
            elif part == 1:
                total[:, at] = total[:, at] + add
            else:
                sk_out[me, :, at] = ((total[:, at] + add) * rowm[...] * colm[:, at]).astype(bf16)

        tiles(width // 256, tile)

    rings = []
    part_rows = rows // SK_PARTS
    for part in range(SK_PARTS):
        view = lambda o, half, part=part: sk_out.at[
            o, pl.ds(part * part_rows, part_rows), pl.ds(half * half_w, half_w)
        ]
        rings.append(ring(view, s_send.at[part], s_recv.at[part]))
    for r in rings:
        r[0]()
    keep.wait()
    for i in range(1, blks):
        o = lax.rem(me + i, blks)
        ref = pieces_out.at[0, o]
        remote(ref, ref, a_send.at[i], a_recv.at[o], up).wait_recv()
    for slot, to in ((0, up), (1, down)):
        go(remote(pieces_out.at[0], pieces_out.at[1 + slot], n_send.at[slot], n_recv.at[slot], to))
    for stage in range(1, 5):
        for r in rings:
            r[stage]()
    for slot in range(2):
        ref = pieces_out.at[1 + slot]
        remote(ref, ref, n_send.at[slot], n_recv.at[slot], up).wait_recv()
    for copy in started:
        copy.wait_send()


def gather_sketched(right, left, gates, sketch, rowm, colm, pieces):
    bf16, f32 = jnp.bfloat16, jnp.float32
    rows, middle = left.shape
    depth, columns = right.shape
    width = sketch.shape[1]
    blks = SIDE * SIDE
    vmem = pl.BlockSpec(memory_space=pltpu.VMEM)
    dma = pltpu.SemaphoreType.DMA
    return pl.pallas_call(
        gather_kernel,
        out_shape=(
            jax.ShapeDtypeStruct((blks, rows, width), bf16),
            jax.ShapeDtypeStruct((3,) + pieces.shape, bf16),
        ),
        in_specs=[vmem, vmem, vmem, pl.BlockSpec(memory_space=pl.ANY), vmem, vmem, vmem],
        out_specs=(vmem, vmem),
        scratch_shapes=[
            pltpu.VMEM((columns, width), bf16),
            pltpu.VMEM((3, blks, depth, width), bf16),
            pltpu.VMEM((2, depth, columns), bf16),
            pltpu.VMEM((2, rows, middle), bf16),
            pltpu.VMEM((rows, width), f32),
            dma(()),
            dma((4,)),
            dma((4,)),
            dma((3, 30)),
            dma((3, 2, blks)),
            dma((SK_PARTS, 30)),
            dma((SK_PARTS, 2, blks)),
            dma((blks,)),
            dma((blks,)),
            dma((2,)),
            dma((2,)),
        ],
        compiler_params=pltpu.CompilerParams(
            collective_id=0, has_side_effects=True, vmem_limit_bytes=48 * 2**20
        ),
    )(right, left, gates, sketch, rowm, colm, pieces)


def body(left_tensor, right_tensor, diag_gate, hop_gate, sketch, sector_rows, kept):
    bf16, f32 = jnp.bfloat16, jnp.float32
    left, right, diag, hop = left_tensor[0], right_tensor[0], diag_gate[0], hop_gate[0]
    rows_here, middle = left.shape
    width = sketch.shape[1]
    depth, columns = right.shape
    blks = lax.axis_size("blk")
    total = rows_here * blks
    cols_here = columns // blks
    g, me = lax.axis_index("grp"), lax.axis_index("blk")
    hop_low = jnp.where(g > 0, hop, 0.0)
    hop_high = jnp.where(g < lax.axis_size("grp") - 1, hop, 0.0)
    gates = jnp.stack([diag, hop_low, hop_high])
    row_index = me * rows_here + jnp.arange(rows_here, dtype=jnp.int32)
    rowm = (row_index[:, None] < sector_rows[0]).astype(f32)
    colm = (jnp.arange(width, dtype=jnp.int32)[None, :] < kept[0]).astype(f32)
    pieces = jnp.concatenate(
        [
            right.reshape(depth, blks, cols_here).transpose(1, 0, 2),
            left.T.reshape(blks, depth, rows_here),
        ],
        axis=1,
    )
    sk, got = gather_sketched(right, left, gates, sketch, rowm, colm, pieces)
    sketched_all = sk.reshape(total, width)
    left_c = got[:, :, depth:, :].transpose(0, 2, 1, 3).reshape(3 * depth, total)
    joint = dot32(left_c, sketched_all, ((1,), (0,))).astype(bf16)
    joint = lax.all_gather(joint.reshape(3, depth, width), "blk", axis=1, tiled=True)
    inverse = factor_inverse(sketched_all, 1.0 - colm)

    gates_c = lax.dynamic_slice_in_dim(gates, me * cols_here, cols_here, axis=1)
    right_c = got[:, :, :depth, :].reshape(3, middle, cols_here)
    right_c = (right_c.astype(f32) * gates_c[:, None, :]).astype(bf16)
    projected = dot32(right_c.reshape(3 * middle, cols_here), joint.reshape(3 * middle, width), ((0,), (0,)))
    scale = math.sqrt(total)
    sketched = lax.dynamic_index_in_dim(sk, me, 0, keepdims=False)
    left_out = dot32(sketched.astype(f32), inverse, ((1,), (1,)), precision=HIGH) * scale
    right_out = dot32(projected, inverse, ((1,), (1,)), precision=HIGH) / scale
    return (left_out[None], right_out[:, None, :])


def solution(mesh):
    in_specs = (
        P("grp", "blk", None),
        P("grp", "blk", None),
        P("grp", None),
        P("grp", None),
        P(),
        P("grp"),
        P("grp"),
    )
    out_specs = (P("grp", "blk", None), P("blk", "grp", None))
    return jax.shard_map(body, mesh=mesh, in_specs=in_specs, out_specs=out_specs, check_vma=False)
```

```python
import math

import jax
import jax.numpy as jnp
from jax import lax
from jax.experimental import pallas as pl
from jax.experimental.pallas import tpu as pltpu
from jax.sharding import PartitionSpec as P

HIGH = lax.Precision.HIGHEST
B = 128
W = 2 * B
SIDE = 4
BLKS = SIDE * SIDE
MESH = pl.DeviceIdType.MESH


def pivot_inverse(a, hooks):
    lane = lax.broadcasted_iota(jnp.int32, (8, B), 1)
    sub = lax.broadcasted_iota(jnp.int32, (8, B), 0)
    n = B // 8
    rest = a.reshape(n, 8, B)
    out = []
    wide = lambda x: jnp.broadcast_to(x, (8, B))
    for q in range(n):
        k = 8 * q
        slab = rest[0]
        cols = [wide(slab[:, k + t : k + t + 1]) for t in range(8)]
        piv = [[wide(cols[j][i : i + 1, :]) if j <= i else None for j in range(8)] for i in range(8)]
        inside = (lane >= k) & (lane < k + 8)
        e = [
            jnp.where(lane == k + t, 1.0, jnp.where(inside, 0.0, wide(slab[t : t + 1, :])))
            for t in range(8)
        ]
        fin, s, u, ds = [None] * 8, [None] * 8, {}, []
        for t in range(0, 8, 2):
            p0, p1, p2 = piv[t][t], piv[t + 1][t], piv[t + 1][t + 1]
            det = p0 * p2 - p1 * p1
            rd = pl.reciprocal(det, approx=True)
            rd = rd * (2.0 - det * rd)
            i0, i1, i2 = p2 * rd, p1 * rd, p0 * rd
            ds.append((i0, i1, i2))
            for i in range(t + 2, 8):
                x0, x1 = piv[i][t], piv[i][t + 1]
                u[i, t] = x0 * i0 - x1 * i1
                u[i, t + 1] = x1 * i2 - x0 * i1
            for i in range(t + 2, 8):
                for j in range(t + 2, i + 1):
                    piv[i][j] = piv[i][j] - (u[i, t] * piv[j][t] + u[i, t + 1] * piv[j][t + 1])
                e[i] = e[i] - (u[i, t] * e[t] + u[i, t + 1] * e[t + 1])
            ra = lax.rsqrt(p0)
            m = p1 * ra * ra
            fin[t] = e[t] * ra
            fin[t + 1] = (e[t + 1] - m * e[t]) * lax.rsqrt(p2 - m * p1)
        if q < n - 1:
            for t in range(6, -1, -2):
                i0, i1, i2 = ds[t // 2]
                v0 = e[t] * i0 - e[t + 1] * i1
                v1 = e[t + 1] * i2 - e[t] * i1
                for i in range(7, t + 1, -1):
                    v0 = v0 - u[i, t] * s[i]
                    v1 = v1 - u[i, t + 1] * s[i]
                s[t], s[t + 1] = v0, v1
            rest = rest[1:]
            new = jnp.where(inside[None], 0.0, rest)
            for t in range(8):
                new = new - jnp.broadcast_to(rest[:, :, k + t : k + t + 1], rest.shape) * s[t][None]
            rest = new
        o = fin[0]
        for t in range(1, 8):
            o = jnp.where(sub == t, fin[t], o)
        out.append(jnp.where(lane <= sub + k, o, 0.0))
        if q in hooks:
            hooks[q]()
    return jnp.concatenate(out, axis=0)


def remote(src, dst, send, recv, to):
    return pltpu.make_async_remote_copy(
        src_ref=src, dst_ref=dst, send_sem=send, recv_sem=recv, device_id=to, device_id_type=MESH
    )


class Ring:
    def __init__(self, buf, split, send, recv, cx, cy, me):
        self.buf, self.split, self.send, self.recv = buf, split, send, recv
        self.cx, self.cy, self.me = cx, cy, me
        self.half_of = {}

    def view(self, c, owner, half):
        rows = self.buf.shape[2]
        at = pl.ds(0, self.split) if half == 0 else pl.ds(self.split, rows - self.split)
        return self.buf.at[c, owner, at, :]

    def owner(self, half, r1, r2):
        c1, c2 = (self.cx, self.cy) if half == 0 else (self.cy, self.cx)
        a, b = lax.rem(c1 + r1, SIDE), lax.rem(c2 + r2, SIDE)
        return a * SIDE + b if half == 0 else b * SIDE + a

    def ship(self, c, half, block, axis, step):
        to = self.owner(half, step, 0) if axis == 0 else self.owner(half, 0, step)
        ref = self.view(c, block, half)
        n = self.count
        self.count += 1
        self.half_of[n] = half
        remote(ref, ref, self.send.at[c, n], self.recv.at[c, half, block], {"blk": to}).start()

    def take(self, c, half, r1, r2):
        block = self.owner(half, r1, r2)
        ref = self.view(c, block, half)
        other = {"blk": lax.rem(self.me + 1, BLKS)}
        remote(ref, ref, self.send.at[c, 0], self.recv.at[c, half, block], other).wait_recv()
        return block

    def relay(self, c, half, r1):
        low = self.take(c, half, r1, 3)
        if r1 in (0, 3):
            self.ship(c, half, low, 1, 1)
        high = self.take(c, half, r1, 1)
        if r1 in (1, 2):
            self.ship(c, half, high, 1, 3)

    def spread(self, c, half, block):
        self.ship(c, half, block, 1, 1)
        self.ship(c, half, block, 1, 3)

    def stage(self, c, k):
        if k == 0:
            self.count = 0
            for half in range(2):
                self.ship(c, half, self.me, 0, 1)
                self.ship(c, half, self.me, 0, 3)
            for half in range(2):
                self.spread(c, half, self.me)
        elif k == 1:
            self.count = 8
            for half in range(2):
                b = self.take(c, half, 3, 0)
                if half == 0:
                    self.ship(c, half, b, 0, 1)
                self.spread(c, half, b)
                b = self.take(c, half, 1, 0)
                if half == 1:
                    self.ship(c, half, b, 0, 3)
                self.spread(c, half, b)
            for half in range(2):
                self.relay(c, half, 0)
        elif k == 2:
            self.count = 20
            for half in range(2):
                self.spread(c, half, self.take(c, half, 2, 0))
            for half in range(2):
                self.relay(c, half, 3)
                self.relay(c, half, 1)
        elif k == 3:
            self.count = 28
            for half in range(2):
                self.relay(c, half, 2)
        else:
            for half in range(2):
                for r1 in (0, 3, 1, 2):
                    self.take(c, half, r1, 2)

    def drain(self, c):
        other = {"blk": lax.rem(self.me + 1, BLKS)}
        for n in range(30):
            ref = self.view(c, self.me, self.half_of[n])
            remote(ref, ref, self.send.at[c, n], self.recv.at[c, 0, 0], other).wait_send()


def dot(a, b, ca, cb, **kw):
    return lax.dot_general(
        a, b, (((ca,), (cb,)), ((), ())), preferred_element_type=jnp.float32, **kw
    )


def bond_kernel(
    right, left, gates, sketch_hbm, rowm, colm,
    inverse, projected, own_out,
    sketch, stack, mapped, sk, sk_t, joint, right_n, left_n, pieces, got, gates_c, left_t, right_t,
    xcol,
    load_sem, keep_sem, x_send, x_recv, m_send, m_recv, s_send, s_recv, j_send, j_recv,
    a_send, a_recv, n_send, n_recv,
):
    bf16, f32 = jnp.bfloat16, jnp.float32
    g = lax.axis_index("grp")
    me = lax.axis_index("blk")
    groups = lax.axis_size("grp")
    depth, columns = right.shape
    rows, middle = left.shape
    chunks = sk.shape[0]
    total = rows * BLKS
    cols_here = columns // BLKS
    up = {"grp": lax.rem(g + 1, groups)}
    down = {"grp": lax.rem(g + groups - 1, groups)}

    load = pltpu.make_async_copy(sketch_hbm, sketch, load_sem)
    load.start()
    barrier = pltpu.get_barrier_semaphore()
    for peer in [{"blk": lax.rem(me + i, BLKS)} for i in range(1, BLKS)] + [up, down]:
        pl.semaphore_signal(barrier, inc=1, device_id=peer, device_id_type=MESH)
    pl.semaphore_wait(barrier, BLKS + 1)

    started = []

    def go(copy):
        copy.start()
        started.append(copy)

    def x_wait(ref, k):
        remote(ref, ref, x_send.at[k], x_recv.at[k], up).wait_recv()

    for slot, to in ((0, up), (1, down)):
        go(remote(right, right_n.at[slot], x_send.at[slot], x_recv.at[slot], to))
    for slot, to in ((0, up), (1, down)):
        go(remote(left, left_n.at[slot], x_send.at[2 + slot], x_recv.at[2 + slot], to))

    turned = left[...].astype(f32).T.astype(bf16).reshape(BLKS, depth, rows)
    for o in range(BLKS):
        pieces[o, 0:depth, :] = right[:, o * cols_here : (o + 1) * cols_here]
        pieces[o, depth : 2 * depth, :] = turned[o]
        gates_c[o] = gates[:, o * cols_here : (o + 1) * cols_here]
    for i in range(1, BLKS):
        to = lax.rem(me + i, BLKS)
        go(remote(pieces.at[to], got.at[0, me], a_send.at[i], a_recv.at[me], {"blk": to}))
    keep = pltpu.make_async_copy(pieces.at[me], got.at[0, me], keep_sem)
    keep.start()

    cx, cy = me // SIDE, me % SIDE
    ring_m = Ring(mapped, 80, m_send, m_recv, cx, cy, me)
    ring_s = Ring(sk, rows // 2, s_send, s_recv, cx, cy, me)
    ring_j = Ring(joint, 80, j_send, j_recv, cx, cy, me)

    def at(c):
        return slice(c * W, (c + 1) * W)

    def make_mapped(c):
        return dot(stack[...], sketch[:, at(c)], 1, 0).astype(bf16)

    def part(buf, c, t):
        return buf[c, :, t * depth : (t + 1) * depth, :].reshape(BLKS * depth, W)

    def make_sketched(c):
        add = dot(left[...], part(mapped, c, 0), 1, 0)
        add = add + dot(left_n[0], part(mapped, c, 1), 1, 0)
        add = add + dot(left_n[1], part(mapped, c, 2), 1, 0)
        return (add * rowm[...] * colm[c]).astype(bf16)

    def make_joint(c):
        return dot(left_t[...], sk[c].reshape(total, W), 1, 0).astype(bf16)

    def project(c):
        add = dot(right_t[0], part(joint, c, 0), 1, 0)
        add = add + dot(right_t[1], part(joint, c, 1), 1, 0)
        projected[:, at(c)] = add + dot(right_t[2], part(joint, c, 2), 1, 0)

    load.wait()
    stack[0:depth, :] = (right[...].astype(f32) * gates[0:1, :]).astype(bf16)
    for slot in range(2):
        x_wait(right_n.at[slot], slot)
        stack[(slot + 1) * depth : (slot + 2) * depth, :] = (
            right_n[slot].astype(f32) * gates[slot + 1 : slot + 2, :]
        ).astype(bf16)

    def start_mapped(c):
        mapped[c, me] = make_mapped(c)
        ring_m.stage(c, 0)

    def start_sketched(c):
        sk[c, me] = make_sketched(c)
        ring_s.stage(c, 0)

    def advance(ring, *pairs):
        for c, k in pairs:
            ring.stage(c, k)

    def pieces_in():
        keep.wait()
        for i in range(1, BLKS):
            o = lax.rem(me + i, BLKS)
            ref = got.at[0, o]
            remote(ref, ref, a_send.at[i], a_recv.at[o], {"blk": o}).wait_recv()
        for slot, to in ((0, up), (1, down)):
            go(remote(got.at[0], got.at[1 + slot], n_send.at[slot], n_recv.at[slot], to))

    def pieces_done():
        for slot in range(2):
            ref = got.at[1 + slot]
            remote(ref, ref, n_send.at[slot], n_recv.at[slot], up).wait_recv()
        mine = gates_c[me]
        for t in range(3):
            both = got[t]
            scaled = both[:, :depth].reshape(middle, cols_here).astype(f32) * mine[t : t + 1, :]
            right_t[t] = scaled.T.astype(bf16)
            for o in range(0, BLKS, 2):
                left_t[t * depth : (t + 1) * depth, o * rows : (o + 2) * rows] = jnp.concatenate(
                    [both[o, depth:], both[o + 1, depth:]], axis=1
                )

    start_mapped(0)
    start_mapped(1)
    advance(ring_m, (0, 1))
    start_mapped(2)
    advance(ring_m, (1, 1))
    advance(ring_m, (0, 2), (1, 2), (2, 1))
    pieces_in()
    advance(ring_m, (0, 3), (1, 3), (2, 2))
    for slot in range(2):
        x_wait(left_n.at[slot], 2 + slot)
    advance(ring_m, (0, 4))
    start_sketched(0)
    advance(ring_m, (1, 4), (2, 3))
    start_sketched(1)
    advance(ring_s, (0, 1))
    inverse[...] = jnp.zeros_like(inverse)
    advance(ring_m, (2, 4))
    advance(ring_s, (0, 2), (1, 1))
    start_sketched(2)
    pieces_done()
    advance(ring_s, (0, 3), (1, 2), (2, 1))

    def start_joint(c):
        joint[c, me] = make_joint(c)
        ring_j.stage(c, 0)

    def finish_joint(c):
        ring_j.stage(c, 4)
        project(c)

    M, S, J = (lambda c, k, r=r: (r.stage, c, k) for r in (ring_m, ring_s, ring_j))
    even = {
        0: [S(0, 4), S(1, 3), S(2, 2)],
        1: [S(2, 4), J(0, 1)],
        2: [J(0, 3), J(1, 1), (start_joint, 2)],
        3: [J(1, 3), J(2, 2)],
        4: [(finish_joint, 2)],
    }
    odd = {
        0: [S(1, 4), S(2, 3), (start_joint, 0)],
        1: [(start_joint, 1), J(0, 2)],
        2: [(finish_joint, 0), J(1, 2), J(2, 1)],
        3: [(finish_joint, 1), J(2, 3)],
    }

    def run(c, table):
        for cc, todo in table.items():

            @pl.when(c == cc)
            def _(todo=todo):
                for f, *args in todo:
                    f(*args)

    eye = lax.broadcasted_iota(jnp.int32, (B, B), 0) == lax.broadcasted_iota(jnp.int32, (B, B), 1)

    blocks = chunks * (W // B)

    def step(c, carry):
        here = pl.multiple_of(c * B, B)
        ch = c // 2
        off = pl.multiple_of((c % 2) * B, B)
        run(c, even)

        @pl.when(c % 2 == 0)
        def _():
            sk_t[pl.ds(here, W), :] = sk[ch].reshape(total, W).astype(f32).T.astype(bf16)

            def gram(i, cc):
                ii = pl.multiple_of(i * W, W)
                xcol[pl.ds(ii, W), :] = dot(sk_t[pl.ds(ii, W), :], sk[ch].reshape(total, W), 1, 0)
                return cc

            lax.fori_loop(0, ch + 1, gram, 0)

        for cc in range(1, blocks):

            @pl.when(c == cc)
            def _(k=cc * B, mine=slice((cc % 2) * B, (cc % 2 + 1) * B)):
                x = dot(inverse[0:k, 0:k], xcol[0:k, mine], 1, 0, precision=HIGH)
                xt = x.T
                xcol[k : k + B, mine] = xcol[k : k + B, mine] - dot(xt, x, 1, 0, precision=HIGH)
                inverse[k : k + B, 0:k] = dot(xt, inverse[0:k, 0:k], 1, 0, precision=HIGH)

        a = xcol[pl.ds(here, B), pl.ds(off, B)] + jnp.where(eye, 1.0 - colm[ch, :, pl.ds(off, B)], 0.0)
        inv = pivot_inverse(a, {9: lambda: run(c, odd)})
        for cc in range(1, blocks):

            @pl.when(c == cc)
            def _(k=cc * B):
                inverse[k : k + B, 0:k] = -dot(inv, inverse[k : k + B, 0:k], 1, 0, precision=HIGH)

        inverse[pl.ds(here, B), pl.ds(here, B)] = inv
        return carry

    lax.fori_loop(0, blocks, step, 0)
    for c in range(chunks):
        own_out[:, c * W : (c + 1) * W] = sk[c, me]

    def drain(c, carry):
        ring_m.drain(c)
        ring_s.drain(c)
        ring_j.drain(c)
        return carry

    lax.fori_loop(0, chunks, drain, 0)
    for copy in started:
        copy.wait_send()


def bond(right, left, gates, sketch, rowm, colm):
    bf16, f32 = jnp.bfloat16, jnp.float32
    rows, middle = left.shape
    depth, columns = right.shape
    width = sketch.shape[1]
    chunks = width // W
    cols_here = columns // BLKS
    vmem = pl.BlockSpec(memory_space=pltpu.VMEM)
    dma = pltpu.SemaphoreType.DMA
    return pl.pallas_call(
        bond_kernel,
        out_shape=(
            jax.ShapeDtypeStruct((width, width), f32),
            jax.ShapeDtypeStruct((cols_here, width), f32),
            jax.ShapeDtypeStruct((rows, width), bf16),
        ),
        in_specs=[vmem, vmem, vmem, pl.BlockSpec(memory_space=pl.ANY), vmem, vmem],
        out_specs=(vmem, vmem, vmem),
        scratch_shapes=[
            pltpu.VMEM((columns, width), bf16),
            pltpu.VMEM((3 * depth, columns), bf16),
            pltpu.VMEM((chunks, BLKS, 3 * depth, W), bf16),
            pltpu.VMEM((chunks, BLKS, rows, W), bf16),
            pltpu.VMEM((width, rows * BLKS), bf16),
            pltpu.VMEM((chunks, BLKS, 3 * depth, W), bf16),
            pltpu.VMEM((2, depth, columns), bf16),
            pltpu.VMEM((2, rows, middle), bf16),
            pltpu.VMEM((BLKS, 2 * depth, rows), bf16),
            pltpu.VMEM((3, BLKS, 2 * depth, rows), bf16),
            pltpu.VMEM((BLKS, 3, cols_here), f32),
            pltpu.VMEM((3 * depth, rows * BLKS), bf16),
            pltpu.VMEM((3, cols_here, middle), bf16),
            pltpu.VMEM((width, W), f32),
            dma(()),
            dma(()),
            dma((4,)),
            dma((4,)),
            dma((chunks, 30)),
            dma((chunks, 2, BLKS)),
            dma((chunks, 30)),
            dma((chunks, 2, BLKS)),
            dma((chunks, 30)),
            dma((chunks, 2, BLKS)),
            dma((BLKS,)),
            dma((BLKS,)),
            dma((2,)),
            dma((2,)),
        ],
        compiler_params=pltpu.CompilerParams(
            collective_id=0, has_side_effects=True, vmem_limit_bytes=50 * 2**20
        ),
    )(right, left, gates, sketch, rowm, colm)


def dot32(a, b, dims, **kw):
    return lax.dot_general(a, b, (dims, ((), ())), preferred_element_type=jnp.float32, **kw)


def body(left_tensor, right_tensor, diag_gate, hop_gate, sketch, sector_rows, kept):
    f32 = jnp.float32
    left, right, diag, hop = left_tensor[0], right_tensor[0], diag_gate[0], hop_gate[0]
    rows_here, middle = left.shape
    width = sketch.shape[1]
    total = rows_here * lax.axis_size("blk")
    g, me = lax.axis_index("grp"), lax.axis_index("blk")
    hop_low = jnp.where(g > 0, hop, 0.0)
    hop_high = jnp.where(g < lax.axis_size("grp") - 1, hop, 0.0)
    gates = jnp.stack([diag, hop_low, hop_high])
    row_index = me * rows_here + jnp.arange(rows_here, dtype=jnp.int32)
    rowm = (row_index[:, None] < sector_rows[0]).astype(f32)
    colm = (jnp.arange(width, dtype=jnp.int32).reshape(-1, 1, W) < kept[0]).astype(f32)
    inverse, projected, sketched = bond(right, left, gates, sketch, rowm, colm)
    scale = math.sqrt(total)
    left_out = dot32(sketched.astype(f32), inverse, ((1,), (1,)), precision=HIGH) * scale
    right_out = dot32(projected, inverse, ((1,), (1,)), precision=HIGH) / scale
    return (left_out[None], right_out[:, None, :])


def solution(mesh):
    in_specs = (
        P("grp", "blk", None),
        P("grp", "blk", None),
        P("grp", None),
        P("grp", None),
        P(),
        P("grp"),
        P("grp"),
    )
    out_specs = (P("grp", "blk", None), P("blk", "grp", None))
    return jax.shard_map(body, mesh=mesh, in_specs=in_specs, out_specs=out_specs, check_vma=False)
```

```python
import math

import jax
import jax.numpy as jnp
from jax import lax
from jax.experimental import pallas as pl
from jax.experimental.pallas import tpu as pltpu
from jax.sharding import PartitionSpec as P

HIGH = lax.Precision.HIGHEST
B = 128
WIDTHS = (B, 2 * B, 3 * B)
SIDE = 4
BLKS = SIDE * SIDE
MESH = pl.DeviceIdType.MESH


def pivot_inverse(a, hooks):
    lane = lax.broadcasted_iota(jnp.int32, (8, B), 1)
    sub = lax.broadcasted_iota(jnp.int32, (8, B), 0)
    n = B // 8
    rest = a.reshape(n, 8, B)
    out = []
    wide = lambda x: jnp.broadcast_to(x, (8, B))
    for q in range(n):
        k = 8 * q
        slab = rest[0]
        cols = [wide(slab[:, k + t : k + t + 1]) for t in range(8)]
        piv = [[wide(cols[j][i : i + 1, :]) if j <= i else None for j in range(8)] for i in range(8)]
        inside = (lane >= k) & (lane < k + 8)
        e = [
            jnp.where(lane == k + t, 1.0, jnp.where(inside, 0.0, wide(slab[t : t + 1, :])))
            for t in range(8)
        ]
        fin, s, u, ds = [None] * 8, [None] * 8, {}, []
        for t in range(0, 8, 2):
            p0, p1, p2 = piv[t][t], piv[t + 1][t], piv[t + 1][t + 1]
            det = p0 * p2 - p1 * p1
            rd = pl.reciprocal(det, approx=True)
            rd = rd * (2.0 - det * rd)
            i0, i1, i2 = p2 * rd, p1 * rd, p0 * rd
            ds.append((i0, i1, i2))
            for i in range(t + 2, 8):
                x0, x1 = piv[i][t], piv[i][t + 1]
                u[i, t] = x0 * i0 - x1 * i1
                u[i, t + 1] = x1 * i2 - x0 * i1
            for i in range(t + 2, 8):
                for j in range(t + 2, i + 1):
                    piv[i][j] = piv[i][j] - (u[i, t] * piv[j][t] + u[i, t + 1] * piv[j][t + 1])
                e[i] = e[i] - (u[i, t] * e[t] + u[i, t + 1] * e[t + 1])
            ra = lax.rsqrt(p0)
            m = p1 * ra * ra
            fin[t] = e[t] * ra
            fin[t + 1] = (e[t + 1] - m * e[t]) * lax.rsqrt(p2 - m * p1)
        if q < n - 1:
            for t in range(6, -1, -2):
                i0, i1, i2 = ds[t // 2]
                v0 = e[t] * i0 - e[t + 1] * i1
                v1 = e[t + 1] * i2 - e[t] * i1
                for i in range(7, t + 1, -1):
                    v0 = v0 - u[i, t] * s[i]
                    v1 = v1 - u[i, t + 1] * s[i]
                s[t], s[t + 1] = v0, v1
            rest = rest[1:]
            new = jnp.where(inside[None], 0.0, rest)
            for t in range(8):
                new = new - jnp.broadcast_to(rest[:, :, k + t : k + t + 1], rest.shape) * s[t][None]
            rest = new
        o = fin[0]
        for t in range(1, 8):
            o = jnp.where(sub == t, fin[t], o)
        out.append(jnp.where(lane <= sub + k, o, 0.0))
        if q in hooks:
            hooks[q]()
    return jnp.concatenate(out, axis=0)


def remote(src, dst, send, recv, to):
    return pltpu.make_async_remote_copy(
        src_ref=src, dst_ref=dst, send_sem=send, recv_sem=recv, device_id=to, device_id_type=MESH
    )


class Ring:
    def __init__(self, buf, split, send, recv, cx, cy, me):
        self.buf, self.split, self.send, self.recv = buf, split, send, recv
        self.cx, self.cy, self.me = cx, cy, me
        self.half_of = {}

    def view(self, c, owner, half):
        rows = self.buf[c].shape[1]
        at = pl.ds(0, self.split) if half == 0 else pl.ds(self.split, rows - self.split)
        return self.buf[c].at[owner, at, :]

    def owner(self, half, r1, r2):
        c1, c2 = (self.cx, self.cy) if half == 0 else (self.cy, self.cx)
        a, b = lax.rem(c1 + r1, SIDE), lax.rem(c2 + r2, SIDE)
        return a * SIDE + b if half == 0 else b * SIDE + a

    def ship(self, c, half, block, axis, step):
        to = self.owner(half, step, 0) if axis == 0 else self.owner(half, 0, step)
        ref = self.view(c, block, half)
        n = self.count
        self.count += 1
        self.half_of[n] = half
        remote(ref, ref, self.send.at[c, n], self.recv.at[c, half, block], {"blk": to}).start()

    def take(self, c, half, r1, r2):
        block = self.owner(half, r1, r2)
        ref = self.view(c, block, half)
        other = {"blk": lax.rem(self.me + 1, BLKS)}
        remote(ref, ref, self.send.at[c, 0], self.recv.at[c, half, block], other).wait_recv()
        return block

    def relay(self, c, half, r1):
        low = self.take(c, half, r1, 3)
        if r1 in (0, 3):
            self.ship(c, half, low, 1, 1)
        high = self.take(c, half, r1, 1)
        if r1 in (1, 2):
            self.ship(c, half, high, 1, 3)

    def spread(self, c, half, block):
        self.ship(c, half, block, 1, 1)
        self.ship(c, half, block, 1, 3)

    def stage(self, c, k):
        if k == 0:
            self.count = 0
            for half in range(2):
                self.ship(c, half, self.me, 0, 1)
                self.ship(c, half, self.me, 0, 3)
            for half in range(2):
                self.spread(c, half, self.me)
        elif k == 1:
            self.count = 8
            for half in range(2):
                b = self.take(c, half, 3, 0)
                if half == 0:
                    self.ship(c, half, b, 0, 1)
                self.spread(c, half, b)
                b = self.take(c, half, 1, 0)
                if half == 1:
                    self.ship(c, half, b, 0, 3)
                self.spread(c, half, b)
            for half in range(2):
                self.relay(c, half, 0)
        elif k == 2:
            self.count = 20
            for half in range(2):
                self.spread(c, half, self.take(c, half, 2, 0))
            for half in range(2):
                self.relay(c, half, 3)
                self.relay(c, half, 1)
        elif k == 3:
            self.count = 28
            for half in range(2):
                self.relay(c, half, 2)
        else:
            for half in range(2):
                for r1 in (0, 3, 1, 2):
                    self.take(c, half, r1, 2)

    def direct(self, c):
        ref = self.buf[c].at[self.me]
        for i in range(1, BLKS):
            to = lax.rem(self.me + i, BLKS)
            remote(ref, ref, self.send.at[c, i], self.recv.at[c, 0, self.me], {"blk": to}).start()

    def direct_done(self, c):
        for i in range(1, BLKS):
            o = lax.rem(self.me + i, BLKS)
            ref = self.buf[c].at[o]
            remote(ref, ref, self.send.at[c, i], self.recv.at[c, 0, o], {"blk": o}).wait_recv()

    def direct_drain(self, c):
        ref = self.buf[c].at[self.me]
        for i in range(1, BLKS):
            o = lax.rem(self.me + i, BLKS)
            remote(ref, ref, self.send.at[c, i], self.recv.at[c, 0, o], {"blk": o}).wait_send()

    def drain(self, c):
        other = {"blk": lax.rem(self.me + 1, BLKS)}
        for n in range(30):
            ref = self.view(c, self.me, self.half_of[n])
            remote(ref, ref, self.send.at[c, n], self.recv.at[c, 0, 0], other).wait_send()


def dot3(a, b):
    f32, bf16 = jnp.float32, jnp.bfloat16
    ah, bh = a.astype(bf16), b.astype(bf16)
    al = (a - ah.astype(f32)).astype(bf16)
    bl = (b - bh.astype(f32)).astype(bf16)
    return dot(ah, bh, 1, 0) + (dot(ah, bl, 1, 0) + dot(al, bh, 1, 0))


def dot(a, b, ca, cb, **kw):
    return lax.dot_general(
        a, b, (((ca,), (cb,)), ((), ())), preferred_element_type=jnp.float32, **kw
    )


def bond_kernel(
    right_hbm, left_hbm, diag_hbm, hop_hbm, sketch_hbm, live_rows, kept,
    inverse, projected, own_out,
    right, left, hop, gates, rowm, colm, sketch, stack, m0, m1, m2, k0, k1, k2, sk_t, j0, j1, j2, right_n, left_n, pieces, got, gates_c, left_t, right_t,
    xcol,
    load_sem, right_sem, left_sem, diag_sem, hop_sem, keep_sem, x_send, x_recv, m_send, m_recv, s_send, s_recv, j_send, j_recv,
    a_send, a_recv, n_send, n_recv,
):
    bf16, f32 = jnp.bfloat16, jnp.float32
    g = lax.axis_index("grp")
    me = lax.axis_index("blk")
    groups = lax.axis_size("grp")
    depth, columns = right.shape
    rows, middle = left.shape
    mapped, sk, joint = (m0, m1, m2), (k0, k1, k2), (j0, j1, j2)
    starts = [sum(WIDTHS[:c]) for c in range(len(WIDTHS))]
    total = rows * BLKS
    cols_here = columns // BLKS
    up = {"grp": lax.rem(g + 1, groups)}
    down = {"grp": lax.rem(g + groups - 1, groups)}

    load = pltpu.make_async_copy(sketch_hbm, sketch, load_sem)
    load_right = pltpu.make_async_copy(right_hbm, right, right_sem)
    load_left = pltpu.make_async_copy(left_hbm, left, left_sem)
    load_right.start()
    load_left.start()
    load_diag = pltpu.make_async_copy(diag_hbm, gates.at[pl.ds(0, 1)], diag_sem)
    load_hop = pltpu.make_async_copy(hop_hbm, hop, hop_sem)
    load_diag.start()
    load_hop.start()
    load.start()
    barrier = pltpu.get_barrier_semaphore()
    for peer in [{"blk": lax.rem(me + i, BLKS)} for i in range(1, BLKS)] + [up, down]:
        pl.semaphore_signal(barrier, inc=1, device_id=peer, device_id_type=MESH)
    load_diag.wait()
    load_hop.wait()
    gates[1:2, :] = jnp.where(g > 0, hop[...], 0.0)
    gates[2:3, :] = jnp.where(g < groups - 1, hop[...], 0.0)
    row = me * rows + lax.broadcasted_iota(jnp.int32, (rows, 1), 0)
    rowm[...] = jnp.where(row < live_rows[0], 1.0, 0.0)
    col = lax.broadcasted_iota(jnp.int32, colm.shape, 1)
    colm[...] = jnp.where(col < kept[0], 1.0, 0.0)
    load_right.wait()
    load_left.wait()
    pl.semaphore_wait(barrier, BLKS + 1)

    started = []

    def go(copy):
        copy.start()
        started.append(copy)

    def x_wait(ref, k):
        remote(ref, ref, x_send.at[k], x_recv.at[k], up).wait_recv()

    for slot, to in ((0, up), (1, down)):
        go(remote(right, right_n.at[slot], x_send.at[slot], x_recv.at[slot], to))
    for slot, to in ((0, up), (1, down)):
        go(remote(left, left_n.at[slot], x_send.at[2 + slot], x_recv.at[2 + slot], to))

    turned = left[...].astype(f32).T.astype(bf16).reshape(BLKS, depth, rows)
    for o in range(BLKS):
        pieces[o] = jnp.concatenate(
            [right[:, o * cols_here : (o + 1) * cols_here], turned[o]], axis=1
        )
        gates_c[o] = gates[:, o * cols_here : (o + 1) * cols_here]
    for i in range(1, BLKS):
        to = lax.rem(me + i, BLKS)
        go(remote(pieces.at[to], got.at[0, me], a_send.at[i], a_recv.at[me], {"blk": to}))
    keep = pltpu.make_async_copy(pieces.at[me], got.at[0, me], keep_sem)
    keep.start()

    cx, cy = me // SIDE, me % SIDE
    ring_m = Ring(mapped, 80, m_send, m_recv, cx, cy, me)
    ring_s = Ring(sk, rows // 2, s_send, s_recv, cx, cy, me)
    ring_j = Ring(joint, 80, j_send, j_recv, cx, cy, me)

    def at(c):
        return slice(starts[c], starts[c] + WIDTHS[c])

    def make_mapped(c):
        return dot(stack[...], sketch[:, at(c)], 1, 0).astype(bf16)

    def part(buf, c, t):
        return buf[c][:, t * depth : (t + 1) * depth, :].reshape(BLKS * depth, WIDTHS[c])

    def make_sketched(c):
        add = dot(left[...], part(mapped, c, 0), 1, 0)
        add = add + dot(left_n[0], part(mapped, c, 1), 1, 0)
        add = add + dot(left_n[1], part(mapped, c, 2), 1, 0)
        return (add * rowm[...] * colm[:, at(c)]).astype(bf16)

    def make_joint(c):
        return dot(left_t[...], sk[c][...].reshape(total, WIDTHS[c]), 1, 0).astype(bf16)

    def project(c):
        add = dot(right_t[0], part(joint, c, 0), 1, 0)
        add = add + dot(right_t[1], part(joint, c, 1), 1, 0)
        projected[:, at(c)] = add + dot(right_t[2], part(joint, c, 2), 1, 0)

    load.wait()
    stack[0:depth, :] = (right[...].astype(f32) * gates[0:1, :]).astype(bf16)
    for slot in range(2):
        x_wait(right_n.at[slot], slot)
        stack[(slot + 1) * depth : (slot + 2) * depth, :] = (
            right_n[slot].astype(f32) * gates[slot + 1 : slot + 2, :]
        ).astype(bf16)

    def start_mapped(c):
        mapped[c][me] = make_mapped(c)
        if c:
            ring_m.stage(c, 0)
        else:
            ring_m.direct(c)

    def start_sketched(c):
        sk[c][me] = make_sketched(c)
        if c:
            ring_s.stage(c, 0)
        else:
            ring_s.direct(c)

    def advance(ring, *pairs):
        for c, k in pairs:
            ring.stage(c, k)

    def pieces_in():
        keep.wait()
        for i in range(1, BLKS):
            o = lax.rem(me + i, BLKS)
            ref = got.at[0, o]
            remote(ref, ref, a_send.at[i], a_recv.at[o], {"blk": o}).wait_recv()
        for slot, to in ((0, up), (1, down)):
            go(remote(got.at[0], got.at[1 + slot], n_send.at[slot], n_recv.at[slot], to))

    def pieces_done():
        for slot in range(2):
            ref = got.at[1 + slot]
            remote(ref, ref, n_send.at[slot], n_recv.at[slot], up).wait_recv()
        mine = gates_c[me]
        for t in range(3):
            both = got[t]
            scaled = both[:, :, :cols_here].reshape(middle, cols_here).astype(f32) * mine[t : t + 1, :]
            right_t[t] = scaled.T.astype(bf16)
            for o in range(0, BLKS, 2):
                left_t[t * depth : (t + 1) * depth, o * rows : (o + 2) * rows] = jnp.concatenate(
                    [both[o, :, cols_here:], both[o + 1, :, cols_here:]], axis=1
                )

    start_mapped(0)
    start_mapped(1)
    advance(ring_m, (1, 1))
    start_mapped(2)
    ring_m.direct_done(0)
    for slot in range(2):
        x_wait(left_n.at[slot], 2 + slot)
    start_sketched(0)
    advance(ring_m, (1, 2), (2, 1))
    inverse[...] = jnp.zeros_like(inverse)
    advance(ring_m, (1, 3), (2, 2))
    advance(ring_m, (1, 4))
    start_sketched(1)
    advance(ring_m, (2, 3))
    pieces_in()
    advance(ring_s, (1, 1))
    advance(ring_m, (2, 4))
    start_sketched(2)

    def start_joint(c):
        joint[c][me] = make_joint(c)
        ring_j.stage(c, 0)

    def finish_joint(c):
        ring_j.stage(c, 4)
        project(c)

    def gram(c):
        w, at0 = WIDTHS[c], starts[c]
        sk_t[at(c), :] = sk[c][...].reshape(total, w).astype(f32).T.astype(bf16)
        for b in range(c + 1):
            xcol[at(b), at(c)] = dot(sk_t[at(b), :], sk[c][...].reshape(total, w), 1, 0)

    M, S, J = (lambda c, k, r=r: (r.stage, c, k) for r in (ring_m, ring_s, ring_j))
    even = {
        0: [(ring_s.direct_done, 0), (gram, 0)],
        1: [S(1, 4), (gram, 1), S(2, 3), (pieces_done,)],
        2: [J(0, 1), (start_joint, 2)],
        3: [(gram, 2), J(0, 3), J(2, 1)],
        4: [J(2, 2)],
        5: [(finish_joint, 1)],
    }
    odd = {
        0: [S(1, 3), S(2, 2)],
        1: [S(2, 4), (start_joint, 0), (start_joint, 1)],
        2: [J(0, 2), J(1, 1)],
        3: [(finish_joint, 0), J(1, 2)],
        4: [J(1, 3), J(2, 3)],
        5: [(finish_joint, 2)],
    }
    first = {0: [S(1, 2), S(2, 1)]}

    def run(c, table):
        for cc, todo in table.items():

            @pl.when(c == cc)
            def _(todo=todo):
                for f, *args in todo:
                    f(*args)

    eye = lax.broadcasted_iota(jnp.int32, (B, B), 0) == lax.broadcasted_iota(jnp.int32, (B, B), 1)

    blocks = sum(WIDTHS) // B

    def step(c, carry):
        here = pl.multiple_of(c * B, B)
        run(c, even)
        for cc in range(1, blocks):

            @pl.when(c == cc)
            def _(k=cc * B, mine=slice(cc * B, (cc + 1) * B)):
                x = dot3(inverse[0:k, 0:k], xcol[0:k, mine])
                xt = x.T
                xcol[k : k + B, mine] = xcol[k : k + B, mine] - dot3(xt, x)
                inverse[k : k + B, 0:k] = dot3(xt, inverse[0:k, 0:k])

        a = xcol[pl.ds(here, B), pl.ds(here, B)] + jnp.where(eye, 1.0 - colm[:, pl.ds(here, B)], 0.0)
        inv = pivot_inverse(a, {2: lambda: run(c, first), 9: lambda: run(c, odd)})
        for cc in range(1, blocks):

            @pl.when(c == cc)
            def _(k=cc * B):
                inverse[k : k + B, 0:k] = -dot3(inv, inverse[k : k + B, 0:k])

        inverse[pl.ds(here, B), pl.ds(here, B)] = inv
        return carry

    lax.fori_loop(0, blocks, step, 0)
    for c in range(len(WIDTHS)):
        own_out[:, at(c)] = sk[c][me]
    ring_m.direct_drain(0)
    ring_s.direct_drain(0)
    ring_j.drain(0)
    for c in range(1, len(WIDTHS)):
        ring_m.drain(c)
        ring_s.drain(c)
        ring_j.drain(c)
    for copy in started:
        copy.wait_send()


def bond(right, left, diag, hop, sketch, live_rows, kept):
    bf16, f32 = jnp.bfloat16, jnp.float32
    rows, middle = left.shape
    depth, columns = right.shape
    width = sketch.shape[1]
    chunks = len(WIDTHS)
    cols_here = columns // BLKS
    vmem = pl.BlockSpec(memory_space=pltpu.VMEM)
    smem = pl.BlockSpec(memory_space=pltpu.SMEM)
    anyw = pl.BlockSpec(memory_space=pl.ANY)
    dma = pltpu.SemaphoreType.DMA
    return pl.pallas_call(
        bond_kernel,
        out_shape=(
            jax.ShapeDtypeStruct((width, width), f32),
            jax.ShapeDtypeStruct((cols_here, width), f32),
            jax.ShapeDtypeStruct((rows, width), bf16),
        ),
        in_specs=[anyw, anyw, anyw, anyw, anyw, smem, smem],
        out_specs=(vmem, vmem, vmem),
        scratch_shapes=[
            pltpu.VMEM((depth, columns), bf16),
            pltpu.VMEM((rows, middle), bf16),
            pltpu.VMEM((1, columns), f32),
            pltpu.VMEM((3, columns), f32),
            pltpu.VMEM((rows, 1), f32),
            pltpu.VMEM((1, width), f32),
            pltpu.VMEM((columns, width), bf16),
            pltpu.VMEM((3 * depth, columns), bf16),
            *(pltpu.VMEM((BLKS, 3 * depth, w), bf16) for w in WIDTHS),
            *(pltpu.VMEM((BLKS, rows, w), bf16) for w in WIDTHS),
            pltpu.VMEM((width, rows * BLKS), bf16),
            *(pltpu.VMEM((BLKS, 3 * depth, w), bf16) for w in WIDTHS),
            pltpu.VMEM((2, depth, columns), bf16),
            pltpu.VMEM((2, rows, middle), bf16),
            pltpu.VMEM((BLKS, depth, cols_here + rows), bf16),
            pltpu.VMEM((3, BLKS, depth, cols_here + rows), bf16),
            pltpu.VMEM((BLKS, 3, cols_here), f32),
            pltpu.VMEM((3 * depth, rows * BLKS), bf16),
            pltpu.VMEM((3, cols_here, middle), bf16),
            pltpu.VMEM((width, width), f32),
            dma(()),
            dma(()),
            dma(()),
            dma(()),
            dma(()),
            dma(()),
            dma((4,)),
            dma((4,)),
            dma((chunks, 30)),
            dma((chunks, 2, BLKS)),
            dma((chunks, 30)),
            dma((chunks, 2, BLKS)),
            dma((chunks, 30)),
            dma((chunks, 2, BLKS)),
            dma((BLKS,)),
            dma((BLKS,)),
            dma((2,)),
            dma((2,)),
        ],
        compiler_params=pltpu.CompilerParams(
            collective_id=0, has_side_effects=True, vmem_limit_bytes=60 * 2**20
        ),
    )(right, left, diag, hop, sketch, live_rows, kept)


def body(left_tensor, right_tensor, diag_gate, hop_gate, sketch, sector_rows, kept):
    f32 = jnp.float32
    inverse, projected, sketched = bond(
        right_tensor[0], left_tensor[0], diag_gate, hop_gate, sketch, sector_rows, kept
    )
    scale = math.sqrt(left_tensor.shape[1] * lax.axis_size("blk"))
    precise = dict(preferred_element_type=f32, precision=lax.Precision.HIGH)
    solve = (((1,), (1,)), ((), ()))
    left_out = lax.dot_general(sketched.astype(f32), inverse, solve, **precise) * scale
    right_out = lax.dot_general(projected, inverse, solve, **precise) / scale
    return (left_out[None], right_out[:, None, :])


def solution(mesh):
    in_specs = (
        P("grp", "blk", None),
        P("grp", "blk", None),
        P("grp", None),
        P("grp", None),
        P(),
        P("grp"),
        P("grp"),
    )
    out_specs = (P("grp", "blk", None), P("blk", "grp", None))
    return jax.shard_map(body, mesh=mesh, in_specs=in_specs, out_specs=out_specs, check_vma=False)
```

```python
import math

import jax
import jax.numpy as jnp
from jax import lax
from jax.experimental import pallas as pl
from jax.experimental.pallas import tpu as pltpu
from jax.sharding import PartitionSpec as P

HIGH = lax.Precision.HIGHEST
B = 128
WIDTHS = (B, 3 * B, 2 * B)
SIDE = 4
BLKS = SIDE * SIDE
MESH = pl.DeviceIdType.MESH


def pivot_inverse(a, hooks):
    lane = lax.broadcasted_iota(jnp.int32, (8, B), 1)
    sub = lax.broadcasted_iota(jnp.int32, (8, B), 0)
    n = B // 8
    rest = a.reshape(n, 8, B)
    out = []
    wide = lambda x: jnp.broadcast_to(x, (8, B))
    for q in range(n):
        k = 8 * q
        slab = rest[0]
        cols = [wide(slab[:, k + t : k + t + 1]) for t in range(8)]
        piv = [[wide(cols[j][i : i + 1, :]) if j <= i else None for j in range(8)] for i in range(8)]
        inside = (lane >= k) & (lane < k + 8)
        e = [
            jnp.where(lane == k + t, 1.0, jnp.where(inside, 0.0, wide(slab[t : t + 1, :])))
            for t in range(8)
        ]
        fin, s, u, ds = [None] * 8, [None] * 8, {}, []
        for t in range(0, 8, 2):
            p0, p1, p2 = piv[t][t], piv[t + 1][t], piv[t + 1][t + 1]
            det = p0 * p2 - p1 * p1
            rd = pl.reciprocal(det, approx=True)
            rd = rd * (2.0 - det * rd)
            i0, i1, i2 = p2 * rd, p1 * rd, p0 * rd
            ds.append((i0, i1, i2))
            for i in range(t + 2, 8):
                x0, x1 = piv[i][t], piv[i][t + 1]
                u[i, t] = x0 * i0 - x1 * i1
                u[i, t + 1] = x1 * i2 - x0 * i1
            for i in range(t + 2, 8):
                for j in range(t + 2, i + 1):
                    piv[i][j] = piv[i][j] - (u[i, t] * piv[j][t] + u[i, t + 1] * piv[j][t + 1])
                e[i] = e[i] - (u[i, t] * e[t] + u[i, t + 1] * e[t + 1])
            ra = lax.rsqrt(p0)
            m = p1 * ra * ra
            fin[t] = e[t] * ra
            fin[t + 1] = (e[t + 1] - m * e[t]) * lax.rsqrt(p2 - m * p1)
        if q < n - 1:
            for t in range(6, -1, -2):
                i0, i1, i2 = ds[t // 2]
                v0 = e[t] * i0 - e[t + 1] * i1
                v1 = e[t + 1] * i2 - e[t] * i1
                for i in range(7, t + 1, -1):
                    v0 = v0 - u[i, t] * s[i]
                    v1 = v1 - u[i, t + 1] * s[i]
                s[t], s[t + 1] = v0, v1
            rest = rest[1:]
            new = jnp.where(inside[None], 0.0, rest)
            for t in range(8):
                new = new - jnp.broadcast_to(rest[:, :, k + t : k + t + 1], rest.shape) * s[t][None]
            rest = new
        o = fin[0]
        for t in range(1, 8):
            o = jnp.where(sub == t, fin[t], o)
        out.append(jnp.where(lane <= sub + k, o, 0.0))
        if q in hooks:
            hooks[q]()
    return jnp.concatenate(out, axis=0)


def remote(src, dst, send, recv, to):
    return pltpu.make_async_remote_copy(
        src_ref=src, dst_ref=dst, send_sem=send, recv_sem=recv, device_id=to, device_id_type=MESH
    )


class Ring:
    def __init__(self, buf, split, send, recv, cx, cy, me):
        self.buf, self.split, self.send, self.recv = buf, split, send, recv
        self.cx, self.cy, self.me = cx, cy, me
        self.half_of = {}

    def view(self, c, owner, half):
        rows = self.buf[c].shape[1]
        at = pl.ds(0, self.split) if half == 0 else pl.ds(self.split, rows - self.split)
        return self.buf[c].at[owner, at, :]

    def owner(self, half, r1, r2):
        c1, c2 = (self.cx, self.cy) if half == 0 else (self.cy, self.cx)
        a, b = lax.rem(c1 + r1, SIDE), lax.rem(c2 + r2, SIDE)
        return a * SIDE + b if half == 0 else b * SIDE + a

    def ship(self, c, half, block, axis, step):
        to = self.owner(half, step, 0) if axis == 0 else self.owner(half, 0, step)
        ref = self.view(c, block, half)
        n = self.count
        self.count += 1
        self.half_of[n] = half
        remote(ref, ref, self.send.at[c, n], self.recv.at[c, half, block], {"blk": to}).start()

    def take(self, c, half, r1, r2):
        block = self.owner(half, r1, r2)
        ref = self.view(c, block, half)
        other = {"blk": lax.rem(self.me + 1, BLKS)}
        remote(ref, ref, self.send.at[c, 0], self.recv.at[c, half, block], other).wait_recv()
        return block

    def relay(self, c, half, r1):
        low = self.take(c, half, r1, 3)
        if r1 in (0, 3):
            self.ship(c, half, low, 1, 1)
        high = self.take(c, half, r1, 1)
        if r1 in (1, 2):
            self.ship(c, half, high, 1, 3)

    def spread(self, c, half, block):
        self.ship(c, half, block, 1, 1)
        self.ship(c, half, block, 1, 3)

    def stage(self, c, k):
        if k == 0:
            self.count = 0
            for half in range(2):
                self.ship(c, half, self.me, 0, 1)
                self.ship(c, half, self.me, 0, 3)
            for half in range(2):
                self.spread(c, half, self.me)
        elif k == 1:
            self.count = 8
            for half in range(2):
                b = self.take(c, half, 3, 0)
                if half == 0:
                    self.ship(c, half, b, 0, 1)
                self.spread(c, half, b)
                b = self.take(c, half, 1, 0)
                if half == 1:
                    self.ship(c, half, b, 0, 3)
                self.spread(c, half, b)
            for half in range(2):
                self.relay(c, half, 0)
        elif k == 2:
            self.count = 20
            for half in range(2):
                self.spread(c, half, self.take(c, half, 2, 0))
            for half in range(2):
                self.relay(c, half, 3)
                self.relay(c, half, 1)
        elif k == 3:
            self.count = 28
            for half in range(2):
                self.relay(c, half, 2)
        else:
            for half in range(2):
                for r1 in (0, 3, 1, 2):
                    self.take(c, half, r1, 2)

    def direct(self, c):
        ref = self.buf[c].at[self.me]
        for i in range(1, BLKS):
            to = lax.rem(self.me + i, BLKS)
            remote(ref, ref, self.send.at[c, i], self.recv.at[c, 0, self.me], {"blk": to}).start()

    def direct_done(self, c):
        for i in range(1, BLKS):
            o = lax.rem(self.me + i, BLKS)
            ref = self.buf[c].at[o]
            remote(ref, ref, self.send.at[c, i], self.recv.at[c, 0, o], {"blk": o}).wait_recv()

    def direct_drain(self, c):
        ref = self.buf[c].at[self.me]
        for i in range(1, BLKS):
            o = lax.rem(self.me + i, BLKS)
            remote(ref, ref, self.send.at[c, i], self.recv.at[c, 0, o], {"blk": o}).wait_send()

    def drain(self, c):
        other = {"blk": lax.rem(self.me + 1, BLKS)}
        for n in range(30):
            ref = self.view(c, self.me, self.half_of[n])
            remote(ref, ref, self.send.at[c, n], self.recv.at[c, 0, 0], other).wait_send()


def dot3(a, b):
    f32, bf16 = jnp.float32, jnp.bfloat16
    ah, bh = a.astype(bf16), b.astype(bf16)
    al = (a - ah.astype(f32)).astype(bf16)
    bl = (b - bh.astype(f32)).astype(bf16)
    return dot(ah, bh, 1, 0) + (dot(ah, bl, 1, 0) + dot(al, bh, 1, 0))


def dot(a, b, ca, cb, **kw):
    return lax.dot_general(
        a, b, (((ca,), (cb,)), ((), ())), preferred_element_type=jnp.float32, **kw
    )


def bond_kernel(
    right_hbm, left_hbm, diag_hbm, hop_hbm, sketch_hbm, live_rows, kept,
    inverse, projected, own_out,
    right, left, hop, gates, rowm, colm, sketch, stack, m0, m1, m2, k0, k1, k2, sk_t, j0, j1, j2, right_n, left_n, pieces, got, gates_c, left_t, right_t,
    xcol,
    load_sem, right_sem, left_sem, diag_sem, hop_sem, keep_sem, x_send, x_recv, m_send, m_recv, s_send, s_recv, j_send, j_recv,
    a_send, a_recv, n_send, n_recv,
):
    bf16, f32 = jnp.bfloat16, jnp.float32
    g = lax.axis_index("grp")
    me = lax.axis_index("blk")
    groups = lax.axis_size("grp")
    depth, columns = right.shape
    rows, middle = left.shape
    mapped, sk, joint = (m0, m1, m2), (k0, k1, k2), (j0, j1, j2)
    starts = [sum(WIDTHS[:c]) for c in range(len(WIDTHS))]
    total = rows * BLKS
    cols_here = columns // BLKS
    up = {"grp": lax.rem(g + 1, groups)}
    down = {"grp": lax.rem(g + groups - 1, groups)}

    load = pltpu.make_async_copy(sketch_hbm, sketch, load_sem)
    load_right = pltpu.make_async_copy(right_hbm, right, right_sem)
    load_left = pltpu.make_async_copy(left_hbm, left, left_sem)
    load_right.start()
    load_left.start()
    load_diag = pltpu.make_async_copy(diag_hbm, gates.at[pl.ds(0, 1)], diag_sem)
    load_hop = pltpu.make_async_copy(hop_hbm, hop, hop_sem)
    load_diag.start()
    load_hop.start()
    load.start()
    barrier = pltpu.get_barrier_semaphore()
    for peer in [{"blk": lax.rem(me + i, BLKS)} for i in range(1, BLKS)] + [up, down]:
        pl.semaphore_signal(barrier, inc=1, device_id=peer, device_id_type=MESH)
    load_diag.wait()
    load_hop.wait()
    gates[1:2, :] = jnp.where(g > 0, hop[...], 0.0)
    gates[2:3, :] = jnp.where(g < groups - 1, hop[...], 0.0)
    row = me * rows + lax.broadcasted_iota(jnp.int32, (rows, 1), 0)
    rowm[...] = jnp.where(row < live_rows[0], 1.0, 0.0)
    col = lax.broadcasted_iota(jnp.int32, colm.shape, 1)
    colm[...] = jnp.where(col < kept[0], 1.0, 0.0)
    load_right.wait()
    load_left.wait()
    pl.semaphore_wait(barrier, BLKS + 1)

    started = []

    def go(copy):
        copy.start()
        started.append(copy)

    def x_wait(ref, k):
        remote(ref, ref, x_send.at[k], x_recv.at[k], up).wait_recv()

    for slot, to in ((0, up), (1, down)):
        go(remote(right, right_n.at[slot], x_send.at[slot], x_recv.at[slot], to))
    for slot, to in ((0, up), (1, down)):
        go(remote(left, left_n.at[slot], x_send.at[2 + slot], x_recv.at[2 + slot], to))

    turned = left[...].astype(f32).T.astype(bf16).reshape(BLKS, depth, rows)
    for o in range(BLKS):
        pieces[o] = jnp.concatenate(
            [right[:, o * cols_here : (o + 1) * cols_here], turned[o]], axis=1
        )
        gates_c[o] = gates[:, o * cols_here : (o + 1) * cols_here]
    for i in range(1, BLKS):
        to = lax.rem(me + i, BLKS)
        go(remote(pieces.at[to], got.at[0, me], a_send.at[i], a_recv.at[me], {"blk": to}))
    keep = pltpu.make_async_copy(pieces.at[me], got.at[0, me], keep_sem)
    keep.start()

    cx, cy = me // SIDE, me % SIDE
    ring_m = Ring(mapped, 80, m_send, m_recv, cx, cy, me)
    ring_s = Ring(sk, rows // 2, s_send, s_recv, cx, cy, me)
    ring_j = Ring(joint, 80, j_send, j_recv, cx, cy, me)

    def at(c):
        return slice(starts[c], starts[c] + WIDTHS[c])

    def make_mapped(c):
        return dot(stack[...], sketch[:, at(c)], 1, 0).astype(bf16)

    def part(buf, c, t):
        return buf[c][:, t * depth : (t + 1) * depth, :].reshape(BLKS * depth, WIDTHS[c])

    def make_sketched(c):
        add = dot(left[...], part(mapped, c, 0), 1, 0)
        add = add + dot(left_n[0], part(mapped, c, 1), 1, 0)
        add = add + dot(left_n[1], part(mapped, c, 2), 1, 0)
        return (add * rowm[...] * colm[:, at(c)]).astype(bf16)

    def make_joint(c):
        return dot(left_t[...], sk[c][...].reshape(total, WIDTHS[c]), 1, 0).astype(bf16)

    def project(c):
        add = dot(right_t[0], part(joint, c, 0), 1, 0)
        add = add + dot(right_t[1], part(joint, c, 1), 1, 0)
        projected[:, at(c)] = add + dot(right_t[2], part(joint, c, 2), 1, 0)

    load.wait()
    stack[0:depth, :] = (right[...].astype(f32) * gates[0:1, :]).astype(bf16)
    for slot in range(2):
        x_wait(right_n.at[slot], slot)
        stack[(slot + 1) * depth : (slot + 2) * depth, :] = (
            right_n[slot].astype(f32) * gates[slot + 1 : slot + 2, :]
        ).astype(bf16)

    def start_mapped(c):
        mapped[c][me] = make_mapped(c)
        if c:
            ring_m.stage(c, 0)
        else:
            ring_m.direct(c)

    def start_sketched(c):
        sk[c][me] = make_sketched(c)
        if c:
            ring_s.stage(c, 0)
        else:
            ring_s.direct(c)

    def advance(ring, *pairs):
        for c, k in pairs:
            ring.stage(c, k)

    def pieces_in():
        keep.wait()
        for i in range(1, BLKS):
            o = lax.rem(me + i, BLKS)
            ref = got.at[0, o]
            remote(ref, ref, a_send.at[i], a_recv.at[o], {"blk": o}).wait_recv()
        for slot, to in ((0, up), (1, down)):
            go(remote(got.at[0], got.at[1 + slot], n_send.at[slot], n_recv.at[slot], to))

    def pieces_done():
        for slot in range(2):
            ref = got.at[1 + slot]
            remote(ref, ref, n_send.at[slot], n_recv.at[slot], up).wait_recv()
        mine = gates_c[me]
        for t in range(3):
            both = got[t]
            scaled = both[:, :, :cols_here].reshape(middle, cols_here).astype(f32) * mine[t : t + 1, :]
            right_t[t] = scaled.T.astype(bf16)
            for o in range(0, BLKS, 2):
                left_t[t * depth : (t + 1) * depth, o * rows : (o + 2) * rows] = jnp.concatenate(
                    [both[o, :, cols_here:], both[o + 1, :, cols_here:]], axis=1
                )

    start_mapped(0)
    start_mapped(1)
    advance(ring_m, (1, 1))
    start_mapped(2)
    ring_m.direct_done(0)
    for slot in range(2):
        x_wait(left_n.at[slot], 2 + slot)
    start_sketched(0)
    advance(ring_m, (1, 2), (2, 1))
    pieces_in()
    advance(ring_m, (1, 3), (2, 2), (1, 4))
    start_sketched(1)
    inverse[...] = jnp.zeros_like(inverse)
    advance(ring_m, (2, 3))
    advance(ring_s, (1, 1))
    pieces_done()
    advance(ring_m, (2, 4))
    start_sketched(2)
    advance(ring_s, (1, 2))

    def start_joint(c):
        joint[c][me] = make_joint(c)
        ring_j.stage(c, 0)

    def finish_joint(c):
        ring_j.stage(c, 4)
        project(c)

    def gram(c):
        w, at0 = WIDTHS[c], starts[c]
        sk_t[at(c), :] = sk[c][...].reshape(total, w).astype(f32).T.astype(bf16)
        for b in range(c + 1):
            xcol[at(b), at(c)] = dot(sk_t[at(b), :], sk[c][...].reshape(total, w), 1, 0)

    M, S, J = (lambda c, k, r=r: (r.stage, c, k) for r in (ring_m, ring_s, ring_j))
    def sent():
        for copy in started:
            copy.wait_send()

    def own():
        for c in range(len(WIDTHS)):
            own_out[:, at(c)] = sk[c][me]

    even = {
        0: [(ring_s.direct_done, 0), (gram, 0)],
        1: [S(1, 4), (gram, 1), S(2, 3), (start_joint, 0)],
        2: [J(0, 1), (start_joint, 2), (ring_m.direct_drain, 0), (sent,)],
        3: [J(0, 3), J(2, 1), (ring_m.drain, 1)],
        4: [(gram, 2), J(1, 3), J(2, 2), (ring_s.direct_drain, 0)],
        5: [(finish_joint, 1), (ring_j.drain, 0), (own,)],
    }
    odd = {
        0: [S(1, 3)],
        1: [S(2, 4), (start_joint, 1)],
        2: [J(0, 2), J(1, 1), (ring_m.drain, 2)],
        3: [(finish_joint, 0), J(1, 2), (ring_s.drain, 1)],
        4: [J(2, 3), (ring_s.drain, 2)],
        5: [(ring_j.drain, 1), (finish_joint, 2)],
    }
    first = {0: [S(2, 1)]}
    third = {0: [S(2, 2)]}

    def run(c, table):
        for cc, todo in table.items():

            @pl.when(c == cc)
            def _(todo=todo):
                for f, *args in todo:
                    f(*args)

    eye = lax.broadcasted_iota(jnp.int32, (B, B), 0) == lax.broadcasted_iota(jnp.int32, (B, B), 1)

    blocks = sum(WIDTHS) // B

    def step(c, carry):
        here = pl.multiple_of(c * B, B)
        run(c, even)
        for cc in range(1, blocks):

            @pl.when(c == cc)
            def _(k=cc * B, mine=slice(cc * B, (cc + 1) * B)):
                x = dot3(inverse[0:k, 0:k], xcol[0:k, mine])
                xt = x.T
                xcol[k : k + B, mine] = xcol[k : k + B, mine] - dot3(xt, x)
                inverse[k : k + B, 0:k] = dot3(xt, inverse[0:k, 0:k])

        a = xcol[pl.ds(here, B), pl.ds(here, B)] + jnp.where(eye, 1.0 - colm[:, pl.ds(here, B)], 0.0)
        inv = pivot_inverse(a, {3: lambda: run(c, first), 8: lambda: run(c, odd), 13: lambda: run(c, third)})
        for cc in range(1, blocks):

            @pl.when(c == cc)
            def _(k=cc * B):
                inverse[k : k + B, 0:k] = -dot3(inv, inverse[k : k + B, 0:k])

        inverse[pl.ds(here, B), pl.ds(here, B)] = inv
        return carry

    lax.fori_loop(0, blocks, step, 0)
    ring_j.drain(2)


def bond(right, left, diag, hop, sketch, live_rows, kept):
    bf16, f32 = jnp.bfloat16, jnp.float32
    rows, middle = left.shape
    depth, columns = right.shape
    width = sketch.shape[1]
    chunks = len(WIDTHS)
    cols_here = columns // BLKS
    vmem = pl.BlockSpec(memory_space=pltpu.VMEM)
    smem = pl.BlockSpec(memory_space=pltpu.SMEM)
    anyw = pl.BlockSpec(memory_space=pl.ANY)
    dma = pltpu.SemaphoreType.DMA
    return pl.pallas_call(
        bond_kernel,
        out_shape=(
            jax.ShapeDtypeStruct((width, width), f32),
            jax.ShapeDtypeStruct((cols_here, width), f32),
            jax.ShapeDtypeStruct((rows, width), bf16),
        ),
        in_specs=[anyw, anyw, anyw, anyw, anyw, smem, smem],
        out_specs=(vmem, vmem, vmem),
        scratch_shapes=[
            pltpu.VMEM((depth, columns), bf16),
            pltpu.VMEM((rows, middle), bf16),
            pltpu.VMEM((1, columns), f32),
            pltpu.VMEM((3, columns), f32),
            pltpu.VMEM((rows, 1), f32),
            pltpu.VMEM((1, width), f32),
            pltpu.VMEM((columns, width), bf16),
            pltpu.VMEM((3 * depth, columns), bf16),
            *(pltpu.VMEM((BLKS, 3 * depth, w), bf16) for w in WIDTHS),
            *(pltpu.VMEM((BLKS, rows, w), bf16) for w in WIDTHS),
            pltpu.VMEM((width, rows * BLKS), bf16),
            *(pltpu.VMEM((BLKS, 3 * depth, w), bf16) for w in WIDTHS),
            pltpu.VMEM((2, depth, columns), bf16),
            pltpu.VMEM((2, rows, middle), bf16),
            pltpu.VMEM((BLKS, depth, cols_here + rows), bf16),
            pltpu.VMEM((3, BLKS, depth, cols_here + rows), bf16),
            pltpu.VMEM((BLKS, 3, cols_here), f32),
            pltpu.VMEM((3 * depth, rows * BLKS), bf16),
            pltpu.VMEM((3, cols_here, middle), bf16),
            pltpu.VMEM((width, width), f32),
            dma(()),
            dma(()),
            dma(()),
            dma(()),
            dma(()),
            dma(()),
            dma((4,)),
            dma((4,)),
            dma((chunks, 30)),
            dma((chunks, 2, BLKS)),
            dma((chunks, 30)),
            dma((chunks, 2, BLKS)),
            dma((chunks, 30)),
            dma((chunks, 2, BLKS)),
            dma((BLKS,)),
            dma((BLKS,)),
            dma((2,)),
            dma((2,)),
        ],
        compiler_params=pltpu.CompilerParams(
            collective_id=0, has_side_effects=True, vmem_limit_bytes=60 * 2**20
        ),
    )(right, left, diag, hop, sketch, live_rows, kept)


def body(left_tensor, right_tensor, diag_gate, hop_gate, sketch, sector_rows, kept):
    f32 = jnp.float32
    inverse, projected, sketched = bond(
        right_tensor[0], left_tensor[0], diag_gate, hop_gate, sketch, sector_rows, kept
    )
    scale = math.sqrt(left_tensor.shape[1] * lax.axis_size("blk"))
    precise = dict(preferred_element_type=f32, precision=lax.Precision.HIGH)
    solve = (((1,), (1,)), ((), ()))
    left_out = lax.dot_general(sketched.astype(f32), inverse, solve, **precise) * scale
    right_out = lax.dot_general(projected, inverse, solve, **precise) / scale
    return (left_out[None], right_out[:, None, :])


def solution(mesh):
    in_specs = (
        P("grp", "blk", None),
        P("grp", "blk", None),
        P("grp", None),
        P("grp", None),
        P(),
        P("grp"),
        P("grp"),
    )
    out_specs = (P("grp", "blk", None), P("blk", "grp", None))
    return jax.shard_map(body, mesh=mesh, in_specs=in_specs, out_specs=out_specs, check_vma=False)
```

```python
import math

import jax
import jax.numpy as jnp
from jax import lax
from jax.experimental import pallas as pl
from jax.experimental.pallas import tpu as pltpu
from jax.sharding import PartitionSpec as P

HIGH = lax.Precision.HIGHEST
B = 128
WIDTHS = (B, 3 * B, 2 * B)
SIDE = 4
BLKS = SIDE * SIDE
MESH = pl.DeviceIdType.MESH


def pivot_inverse(a, hooks):
    lane = lax.broadcasted_iota(jnp.int32, (8, B), 1)
    sub = lax.broadcasted_iota(jnp.int32, (8, B), 0)
    n = B // 8
    rest = a.reshape(n, 8, B)
    out = []
    wide = lambda x: jnp.broadcast_to(x, (8, B))
    for q in range(n):
        k = 8 * q
        slab = rest[0]
        cols = [wide(slab[:, k + t : k + t + 1]) for t in range(8)]
        piv = [[wide(cols[j][i : i + 1, :]) if j <= i else None for j in range(8)] for i in range(8)]
        inside = (lane >= k) & (lane < k + 8)
        e = [
            jnp.where(lane == k + t, 1.0, jnp.where(inside, 0.0, wide(slab[t : t + 1, :])))
            for t in range(8)
        ]
        fin, s, u, ds = [None] * 8, [None] * 8, {}, []
        for t in range(0, 8, 2):
            p0, p1, p2 = piv[t][t], piv[t + 1][t], piv[t + 1][t + 1]
            det = p0 * p2 - p1 * p1
            rd = pl.reciprocal(det, approx=True)
            rd = rd * (2.0 - det * rd)
            i0, i1, i2 = p2 * rd, p1 * rd, p0 * rd
            ds.append((i0, i1, i2))
            for i in range(t + 2, 8):
                x0, x1 = piv[i][t], piv[i][t + 1]
                u[i, t] = x0 * i0 - x1 * i1
                u[i, t + 1] = x1 * i2 - x0 * i1
            for i in range(t + 2, 8):
                for j in range(t + 2, i + 1):
                    piv[i][j] = piv[i][j] - (u[i, t] * piv[j][t] + u[i, t + 1] * piv[j][t + 1])
                e[i] = e[i] - (u[i, t] * e[t] + u[i, t + 1] * e[t + 1])
            ra = lax.rsqrt(p0)
            m = p1 * ra * ra
            fin[t] = e[t] * ra
            fin[t + 1] = (e[t + 1] - m * e[t]) * lax.rsqrt(p2 - m * p1)
        if q < n - 1:
            for t in range(6, -1, -2):
                i0, i1, i2 = ds[t // 2]
                v0 = e[t] * i0 - e[t + 1] * i1
                v1 = e[t + 1] * i2 - e[t] * i1
                for i in range(7, t + 1, -1):
                    v0 = v0 - u[i, t] * s[i]
                    v1 = v1 - u[i, t + 1] * s[i]
                s[t], s[t + 1] = v0, v1
            rest = rest[1:]
            new = jnp.where(inside[None], 0.0, rest)
            for t in range(8):
                new = new - jnp.broadcast_to(rest[:, :, k + t : k + t + 1], rest.shape) * s[t][None]
            rest = new
        o = fin[0]
        for t in range(1, 8):
            o = jnp.where(sub == t, fin[t], o)
        out.append(jnp.where(lane <= sub + k, o, 0.0))
        if q in hooks:
            hooks[q]()
    return jnp.concatenate(out, axis=0)


def remote(src, dst, send, recv, to):
    return pltpu.make_async_remote_copy(
        src_ref=src, dst_ref=dst, send_sem=send, recv_sem=recv, device_id=to, device_id_type=MESH
    )


class Ring:
    def __init__(self, buf, split, send, recv, cx, cy, me):
        self.buf, self.split, self.send, self.recv = buf, split, send, recv
        self.cx, self.cy, self.me = cx, cy, me
        self.half_of = {}

    def view(self, c, owner, half):
        rows = self.buf[c].shape[1]
        at = pl.ds(0, self.split) if half == 0 else pl.ds(self.split, rows - self.split)
        return self.buf[c].at[owner, at, :]

    def owner(self, half, r1, r2):
        c1, c2 = (self.cx, self.cy) if half == 0 else (self.cy, self.cx)
        a, b = lax.rem(c1 + r1, SIDE), lax.rem(c2 + r2, SIDE)
        return a * SIDE + b if half == 0 else b * SIDE + a

    def ship(self, c, half, block, axis, step):
        to = self.owner(half, step, 0) if axis == 0 else self.owner(half, 0, step)
        ref = self.view(c, block, half)
        n = self.count
        self.count += 1
        self.half_of[n] = half
        remote(ref, ref, self.send.at[c, n], self.recv.at[c, half, block], {"blk": to}).start()

    def take(self, c, half, r1, r2):
        block = self.owner(half, r1, r2)
        ref = self.view(c, block, half)
        other = {"blk": lax.rem(self.me + 1, BLKS)}
        remote(ref, ref, self.send.at[c, 0], self.recv.at[c, half, block], other).wait_recv()
        return block

    def relay(self, c, half, r1):
        low = self.take(c, half, r1, 3)
        if r1 in (0, 3):
            self.ship(c, half, low, 1, 1)
        high = self.take(c, half, r1, 1)
        if r1 in (1, 2):
            self.ship(c, half, high, 1, 3)

    def spread(self, c, half, block):
        self.ship(c, half, block, 1, 1)
        self.ship(c, half, block, 1, 3)

    def stage(self, c, k):
        if k == 0:
            self.count = 0
            for half in range(2):
                self.ship(c, half, self.me, 0, 1)
                self.ship(c, half, self.me, 0, 3)
            for half in range(2):
                self.spread(c, half, self.me)
        elif k == 1:
            self.count = 8
            for half in range(2):
                b = self.take(c, half, 3, 0)
                if half == 0:
                    self.ship(c, half, b, 0, 1)
                self.spread(c, half, b)
                b = self.take(c, half, 1, 0)
                if half == 1:
                    self.ship(c, half, b, 0, 3)
                self.spread(c, half, b)
            for half in range(2):
                self.relay(c, half, 0)
        elif k == 2:
            self.count = 20
            for half in range(2):
                self.spread(c, half, self.take(c, half, 2, 0))
            for half in range(2):
                self.relay(c, half, 3)
                self.relay(c, half, 1)
        elif k == 3:
            self.count = 28
            for half in range(2):
                self.relay(c, half, 2)
        else:
            for half in range(2):
                for r1 in (0, 3, 1, 2):
                    self.take(c, half, r1, 2)

    def direct(self, c):
        ref = self.buf[c].at[self.me]
        for i in range(1, BLKS):
            to = lax.rem(self.me + i, BLKS)
            remote(ref, ref, self.send.at[c, i], self.recv.at[c, 0, self.me], {"blk": to}).start()

    def direct_done(self, c):
        for i in range(1, BLKS):
            o = lax.rem(self.me + i, BLKS)
            ref = self.buf[c].at[o]
            remote(ref, ref, self.send.at[c, i], self.recv.at[c, 0, o], {"blk": o}).wait_recv()

    def direct_drain(self, c):
        ref = self.buf[c].at[self.me]
        for i in range(1, BLKS):
            o = lax.rem(self.me + i, BLKS)
            remote(ref, ref, self.send.at[c, i], self.recv.at[c, 0, o], {"blk": o}).wait_send()

    def drain(self, c):
        other = {"blk": lax.rem(self.me + 1, BLKS)}
        for n in range(30):
            ref = self.view(c, self.me, self.half_of[n])
            remote(ref, ref, self.send.at[c, n], self.recv.at[c, 0, 0], other).wait_send()


def dot3(a, b):
    f32, bf16 = jnp.float32, jnp.bfloat16
    ah, bh = a.astype(bf16), b.astype(bf16)
    al = (a - ah.astype(f32)).astype(bf16)
    bl = (b - bh.astype(f32)).astype(bf16)
    return dot(ah, bh, 1, 0) + (dot(ah, bl, 1, 0) + dot(al, bh, 1, 0))


def dot(a, b, ca, cb, **kw):
    return lax.dot_general(
        a, b, (((ca,), (cb,)), ((), ())), preferred_element_type=jnp.float32, **kw
    )


def bond_kernel(
    right_hbm, left_hbm, diag_hbm, hop_hbm, sketch_hbm, live_rows, kept,
    inverse, projected, own_out,
    right, left, hop, gates, rowm, colm, sketch, stack, m0, m1, m2, k0, k1, k2, sk_t, j0, j1, j2, right_n, left_n, pieces, got, gates_c, left_t, right_t,
    xcol,
    load_sem, right_sem, left_sem, diag_sem, hop_sem, keep_sem, x_send, x_recv, m_send, m_recv, s_send, s_recv, j_send, j_recv,
    a_send, a_recv, n_send, n_recv,
):
    bf16, f32 = jnp.bfloat16, jnp.float32
    g = lax.axis_index("grp")
    me = lax.axis_index("blk")
    groups = lax.axis_size("grp")
    depth, columns = right.shape
    rows, middle = left.shape
    mapped, sk, joint = (m0, m1, m2), (k0, k1, k2), (j0, j1, j2)
    starts = [sum(WIDTHS[:c]) for c in range(len(WIDTHS))]
    total = rows * BLKS
    cols_here = columns // BLKS
    up = {"grp": lax.rem(g + 1, groups)}
    down = {"grp": lax.rem(g + groups - 1, groups)}

    load = pltpu.make_async_copy(sketch_hbm, sketch, load_sem)
    load_right = pltpu.make_async_copy(right_hbm, right, right_sem)
    load_left = pltpu.make_async_copy(left_hbm, left, left_sem)
    load_right.start()
    load_left.start()
    load_diag = pltpu.make_async_copy(diag_hbm, gates.at[pl.ds(0, 1)], diag_sem)
    load_hop = pltpu.make_async_copy(hop_hbm, hop, hop_sem)
    load_diag.start()
    load_hop.start()
    load.start()
    barrier = pltpu.get_barrier_semaphore()
    for peer in [{"blk": lax.rem(me + i, BLKS)} for i in range(1, BLKS)] + [up, down]:
        pl.semaphore_signal(barrier, inc=1, device_id=peer, device_id_type=MESH)
    load_diag.wait()
    load_hop.wait()
    gates[1:2, :] = jnp.where(g > 0, hop[...], 0.0)
    gates[2:3, :] = jnp.where(g < groups - 1, hop[...], 0.0)
    row = me * rows + lax.broadcasted_iota(jnp.int32, (rows, 1), 0)
    rowm[...] = jnp.where(row < live_rows[0], 1.0, 0.0)
    col = lax.broadcasted_iota(jnp.int32, colm.shape, 1)
    colm[...] = jnp.where(col < kept[0], 1.0, 0.0)
    load_right.wait()
    load_left.wait()
    pl.semaphore_wait(barrier, BLKS + 1)

    started = []

    def go(copy):
        copy.start()
        started.append(copy)

    def x_wait(ref, k):
        remote(ref, ref, x_send.at[k], x_recv.at[k], up).wait_recv()

    for slot, to in ((0, up), (1, down)):
        go(remote(right, right_n.at[slot], x_send.at[slot], x_recv.at[slot], to))
    for slot, to in ((0, up), (1, down)):
        go(remote(left, left_n.at[slot], x_send.at[2 + slot], x_recv.at[2 + slot], to))

    turned = left[...].astype(f32).T.astype(bf16).reshape(BLKS, depth, rows)
    for o in range(BLKS):
        pieces[o] = jnp.concatenate(
            [right[:, o * cols_here : (o + 1) * cols_here], turned[o]], axis=1
        )
        gates_c[o] = gates[:, o * cols_here : (o + 1) * cols_here]
    for i in range(1, BLKS):
        to = lax.rem(me + i, BLKS)
        go(remote(pieces.at[to], got.at[0, me], a_send.at[i], a_recv.at[me], {"blk": to}))
    keep = pltpu.make_async_copy(pieces.at[me], got.at[0, me], keep_sem)
    keep.start()

    cx, cy = me // SIDE, me % SIDE
    ring_m = Ring(mapped, 80, m_send, m_recv, cx, cy, me)
    ring_s = Ring(sk, rows // 2, s_send, s_recv, cx, cy, me)
    ring_j = Ring(joint, 80, j_send, j_recv, cx, cy, me)

    def at(c):
        return slice(starts[c], starts[c] + WIDTHS[c])

    def make_mapped(c):
        return dot(stack[...], sketch[:, at(c)], 1, 0).astype(bf16)

    def part(buf, c, t):
        return buf[c][:, t * depth : (t + 1) * depth, :].reshape(BLKS * depth, WIDTHS[c])

    def make_sketched(c):
        add = dot(left[...], part(mapped, c, 0), 1, 0)
        add = add + dot(left_n[0], part(mapped, c, 1), 1, 0)
        add = add + dot(left_n[1], part(mapped, c, 2), 1, 0)
        return (add * rowm[...] * colm[:, at(c)]).astype(bf16)

    def make_joint(c):
        return dot(left_t[...], sk[c][...].reshape(total, WIDTHS[c]), 1, 0).astype(bf16)

    def project(c):
        add = dot(right_t[0], part(joint, c, 0), 1, 0)
        add = add + dot(right_t[1], part(joint, c, 1), 1, 0)
        projected[:, at(c)] = add + dot(right_t[2], part(joint, c, 2), 1, 0)

    load.wait()
    stack[0:depth, :] = (right[...].astype(f32) * gates[0:1, :]).astype(bf16)
    for slot in range(2):
        x_wait(right_n.at[slot], slot)
        stack[(slot + 1) * depth : (slot + 2) * depth, :] = (
            right_n[slot].astype(f32) * gates[slot + 1 : slot + 2, :]
        ).astype(bf16)

    def start_mapped(c):
        mapped[c][me] = make_mapped(c)
        if c:
            ring_m.stage(c, 0)
        else:
            ring_m.direct(c)

    def start_sketched(c):
        sk[c][me] = make_sketched(c)
        if c:
            ring_s.stage(c, 0)
        else:
            ring_s.direct(c)

    def advance(ring, *pairs):
        for c, k in pairs:
            ring.stage(c, k)

    def pieces_in():
        keep.wait()
        for i in range(1, BLKS):
            o = lax.rem(me + i, BLKS)
            ref = got.at[0, o]
            remote(ref, ref, a_send.at[i], a_recv.at[o], {"blk": o}).wait_recv()
        for slot, to in ((0, up), (1, down)):
            go(remote(got.at[0], got.at[1 + slot], n_send.at[slot], n_recv.at[slot], to))

    def pieces_done():
        for slot in range(2):
            ref = got.at[1 + slot]
            remote(ref, ref, n_send.at[slot], n_recv.at[slot], up).wait_recv()
        mine = gates_c[me]
        for t in range(3):
            both = got[t]
            scaled = both[:, :, :cols_here].reshape(middle, cols_here).astype(f32) * mine[t : t + 1, :]
            right_t[t] = scaled.T.astype(bf16)
            for o in range(0, BLKS, 2):
                left_t[t * depth : (t + 1) * depth, o * rows : (o + 2) * rows] = jnp.concatenate(
                    [both[o, :, cols_here:], both[o + 1, :, cols_here:]], axis=1
                )

    start_mapped(0)
    start_mapped(1)
    advance(ring_m, (1, 1))
    start_mapped(2)
    ring_m.direct_done(0)
    for slot in range(2):
        x_wait(left_n.at[slot], 2 + slot)
    start_sketched(0)
    advance(ring_m, (1, 2), (2, 1))
    pieces_in()
    advance(ring_m, (1, 3), (2, 2), (1, 4))
    start_sketched(1)
    inverse[...] = jnp.zeros_like(inverse)
    advance(ring_m, (2, 3))
    advance(ring_s, (1, 1))
    pieces_done()
    advance(ring_m, (2, 4))
    start_sketched(2)
    advance(ring_s, (1, 2))

    def start_joint(c):
        joint[c][me] = make_joint(c)
        ring_j.stage(c, 0)

    def finish_joint(c):
        ring_j.stage(c, 4)
        project(c)

    def gram(c):
        w, at0 = WIDTHS[c], starts[c]
        sk_t[at(c), :] = sk[c][...].reshape(total, w).astype(f32).T.astype(bf16)
        for b in range(c + 1):
            xcol[at(b), at(c)] = dot(sk_t[at(b), :], sk[c][...].reshape(total, w), 1, 0)

    M, S, J = (lambda c, k, r=r: (r.stage, c, k) for r in (ring_m, ring_s, ring_j))
    def sent():
        for copy in started:
            copy.wait_send()

    def own():
        for c in range(len(WIDTHS)):
            own_out[:, at(c)] = sk[c][me]

    even = {
        0: [(ring_s.direct_done, 0), (gram, 0)],
        1: [S(1, 4), (gram, 1), S(2, 3)],
        2: [(start_joint, 2), (ring_m.direct_drain, 0), (sent,)],
        3: [J(0, 2), J(2, 1), (ring_m.drain, 1)],
        4: [(gram, 2), J(1, 3), J(2, 2), (ring_s.direct_drain, 0)],
        5: [(finish_joint, 0), (finish_joint, 1), (ring_j.drain, 0), (own,)],
    }
    odd = {
        0: [S(1, 3)],
        1: [S(2, 4), (start_joint, 1), (start_joint, 0)],
        2: [J(1, 1), J(0, 1), (ring_m.drain, 2)],
        3: [J(1, 2), J(0, 3), (ring_s.drain, 1)],
        4: [J(2, 3), (ring_s.drain, 2)],
        5: [(ring_j.drain, 1), (finish_joint, 2)],
    }
    first = {0: [S(2, 1)]}
    third = {0: [S(2, 2)]}

    def run(c, table):
        for cc, todo in table.items():

            @pl.when(c == cc)
            def _(todo=todo):
                for f, *args in todo:
                    f(*args)

    eye = lax.broadcasted_iota(jnp.int32, (B, B), 0) == lax.broadcasted_iota(jnp.int32, (B, B), 1)

    blocks = sum(WIDTHS) // B

    def step(c, carry):
        here = pl.multiple_of(c * B, B)
        run(c, even)
        for cc in range(1, blocks):

            @pl.when(c == cc)
            def _(k=cc * B, mine=slice(cc * B, (cc + 1) * B)):
                x = dot3(inverse[0:k, 0:k], xcol[0:k, mine])
                xt = x.T
                xcol[k : k + B, mine] = xcol[k : k + B, mine] - dot3(xt, x)
                inverse[k : k + B, 0:k] = dot3(xt, inverse[0:k, 0:k])

        a = xcol[pl.ds(here, B), pl.ds(here, B)] + jnp.where(eye, 1.0 - colm[:, pl.ds(here, B)], 0.0)
        inv = pivot_inverse(a, {3: lambda: run(c, first), 8: lambda: run(c, odd), 13: lambda: run(c, third)})
        for cc in range(1, blocks):

            @pl.when(c == cc)
            def _(k=cc * B):
                inverse[k : k + B, 0:k] = -dot3(inv, inverse[k : k + B, 0:k])

        inverse[pl.ds(here, B), pl.ds(here, B)] = inv
        return carry

    lax.fori_loop(0, blocks, step, 0)
    ring_j.drain(2)


def bond(right, left, diag, hop, sketch, live_rows, kept):
    bf16, f32 = jnp.bfloat16, jnp.float32
    rows, middle = left.shape
    depth, columns = right.shape
    width = sketch.shape[1]
    chunks = len(WIDTHS)
    cols_here = columns // BLKS
    vmem = pl.BlockSpec(memory_space=pltpu.VMEM)
    smem = pl.BlockSpec(memory_space=pltpu.SMEM)
    anyw = pl.BlockSpec(memory_space=pl.ANY)
    dma = pltpu.SemaphoreType.DMA
    return pl.pallas_call(
        bond_kernel,
        out_shape=(
            jax.ShapeDtypeStruct((width, width), f32),
            jax.ShapeDtypeStruct((cols_here, width), f32),
            jax.ShapeDtypeStruct((rows, width), bf16),
        ),
        in_specs=[anyw, anyw, anyw, anyw, anyw, smem, smem],
        out_specs=(vmem, vmem, vmem),
        scratch_shapes=[
            pltpu.VMEM((depth, columns), bf16),
            pltpu.VMEM((rows, middle), bf16),
            pltpu.VMEM((1, columns), f32),
            pltpu.VMEM((3, columns), f32),
            pltpu.VMEM((rows, 1), f32),
            pltpu.VMEM((1, width), f32),
            pltpu.VMEM((columns, width), bf16),
            pltpu.VMEM((3 * depth, columns), bf16),
            *(pltpu.VMEM((BLKS, 3 * depth, w), bf16) for w in WIDTHS),
            *(pltpu.VMEM((BLKS, rows, w), bf16) for w in WIDTHS),
            pltpu.VMEM((width, rows * BLKS), bf16),
            *(pltpu.VMEM((BLKS, 3 * depth, w), bf16) for w in WIDTHS),
            pltpu.VMEM((2, depth, columns), bf16),
            pltpu.VMEM((2, rows, middle), bf16),
            pltpu.VMEM((BLKS, depth, cols_here + rows), bf16),
            pltpu.VMEM((3, BLKS, depth, cols_here + rows), bf16),
            pltpu.VMEM((BLKS, 3, cols_here), f32),
            pltpu.VMEM((3 * depth, rows * BLKS), bf16),
            pltpu.VMEM((3, cols_here, middle), bf16),
            pltpu.VMEM((width, width), f32),
            dma(()),
            dma(()),
            dma(()),
            dma(()),
            dma(()),
            dma(()),
            dma((4,)),
            dma((4,)),
            dma((chunks, 30)),
            dma((chunks, 2, BLKS)),
            dma((chunks, 30)),
            dma((chunks, 2, BLKS)),
            dma((chunks, 30)),
            dma((chunks, 2, BLKS)),
            dma((BLKS,)),
            dma((BLKS,)),
            dma((2,)),
            dma((2,)),
        ],
        compiler_params=pltpu.CompilerParams(
            collective_id=0, has_side_effects=True, vmem_limit_bytes=60 * 2**20
        ),
    )(right, left, diag, hop, sketch, live_rows, kept)


def body(left_tensor, right_tensor, diag_gate, hop_gate, sketch, sector_rows, kept):
    f32 = jnp.float32
    inverse, projected, sketched = bond(
        right_tensor[0], left_tensor[0], diag_gate, hop_gate, sketch, sector_rows, kept
    )
    scale = math.sqrt(left_tensor.shape[1] * lax.axis_size("blk"))
    precise = dict(preferred_element_type=f32, precision=lax.Precision.HIGH)
    solve = (((1,), (1,)), ((), ()))
    left_out = lax.dot_general(sketched.astype(f32), inverse, solve, **precise) * scale
    right_out = lax.dot_general(projected, inverse, solve, **precise) / scale
    return (left_out[None], right_out[:, None, :])


def solution(mesh):
    in_specs = (
        P("grp", "blk", None),
        P("grp", "blk", None),
        P("grp", None),
        P("grp", None),
        P(),
        P("grp"),
        P("grp"),
    )
    out_specs = (P("grp", "blk", None), P("blk", "grp", None))
    return jax.shard_map(body, mesh=mesh, in_specs=in_specs, out_specs=out_specs, check_vma=False)
```
